512 devices in a mesh: samp: 64 (over y, z_lo, core), feat: 8 (over z_hi, x).
Axes of the slice: x: 4, y: 4, z: 16 (z_hi: 2, z_lo: 8; z = z_hi * 8 + z_lo), core: 2. Of those that a mesh axis runs over, the one named last changes fastest.
Arguments:
- grads: bfloat16 [32768, 4096], P('samp', 'feat'), may hold values from -60 to 60
- weights: float32 [32768], P('samp'), may hold values from 0.05 to 6
- targets: float32 [4096, 64], P('feat'), may hold values from -6 to 6
Outputs:
- scores: float32 [32768, 64], P(('samp', 'feat'))
- solution: float32 [4096, 64], P('feat')
- residual: float32 [4096, 64], P('feat')
The draws below stay inside these ranges and needn't reach their ends.
All inputs are finite; a program needn't handle non-finite values.
Results may differ from the reference program's by a relative error of at most 0.014.
Values may be sent and summed in bfloat16 or wider, within the bound.
No kernel may reach another device: no remote copies, remote signals or barrier semaphores. Data moves between devices by JAX's collectives and lax.ppermute only.
A program may use at most 64 MiB of HBM per device.

```python
import math
import jax
import jax.numpy as jnp
from jax import lax

FEATURES = 4096
DIRS = 64
ITERS = 2
SAMPLES = 32768


def draw_grads(key, part):
    first = jax.random.fold_in(key, 11)
    second = jax.random.fold_in(key, 12)
    ramp = 1.0 + 2.0 * jnp.arange(FEATURES, dtype=jnp.float32) / FEATURES
    column_scale = jnp.exp(jax.random.uniform(second, (FEATURES,), jnp.float32, math.log(0.1), math.log(3.0))) * ramp
    base = jax.random.normal(first, (SAMPLES, FEATURES), jnp.float32)
    return (base * column_scale[None, :]).astype(jnp.bfloat16)


def draw_weights(key, part):
    first = jax.random.fold_in(key, 21)
    ramp = 1.0 + 2.0 * jnp.arange(SAMPLES, dtype=jnp.float32) / SAMPLES
    base = jnp.exp(jax.random.uniform(first, (SAMPLES,), jnp.float32, math.log(0.05), math.log(2.0)))
    return base * ramp


def block_scale(own_key, dims, shards, low, high):
    def one(position, parts):
        heights = jax.random.uniform(jax.random.fold_in(jax.random.fold_in(own_key, 6), position), (parts,), jnp.float32, low / len(shards), high / len(shards))
        return jnp.repeat(jnp.exp(heights), dims[position] // parts).reshape((-1,) + (1,) * (len(dims) - position - 1))

    factor_of = one(*shards[0])
    for cut in shards[1:]:
        factor_of = factor_of * one(*cut)
    return factor_of


def normal_values(stream_key, dims, deviation, limit, cuts=(), kind=jnp.bfloat16):
    loudness = block_scale(stream_key, dims, cuts, -0.22, 0.18) if cuts else 1.0
    entries = jax.random.normal(stream_key, dims, jnp.float32) * deviation * loudness
    return jnp.minimum(jnp.maximum(entries, -limit), limit).astype(kind)


def setup_inputs(seed: int = 0) -> dict:
    keys = jax.random.split(jax.random.key(seed), 4)
    return {
        "grads": draw_grads(jax.random.fold_in(keys[3], 71), 0),
        "weights": draw_weights(jax.random.fold_in(keys[3], 71), 0),
        "targets": normal_values(keys[2], (FEATURES, DIRS), 1.0, 6.0, ((0, 8),), jnp.float32),
    }


damping_term = 0.1

def apply_operator(grads, weights, vector):
    packed = vector.astype(jnp.bfloat16)
    sample_rows = jnp.dot(grads, packed, preferred_element_type=jnp.float32)
    weighted = (sample_rows * (weights / SAMPLES)[:, None]).astype(jnp.bfloat16)
    image = lax.dot_general(grads, weighted, (((0,), (0,)), ((), ())), preferred_element_type=jnp.float32)
    return (sample_rows, image + damping_term * vector)

def reference(grads, weights, targets):
    solution = jnp.zeros_like(targets)
    resid = targets
    direction = targets
    accum = jnp.zeros((grads.shape[0], targets.shape[1]), jnp.float32)
    norm_now = lax.optimization_barrier(jnp.sum(resid * resid, axis=0))
    for step in range(ITERS):
        sample_rows, image = apply_operator(grads, weights, direction)
        alpha = norm_now / lax.optimization_barrier(jnp.sum(direction * image, axis=0))
        solution = solution + alpha * direction
        resid = resid - alpha * image
        accum = accum + alpha * sample_rows
        if step + 1 < ITERS:
            norm_next = lax.optimization_barrier(jnp.sum(resid * resid, axis=0))
            direction = resid + norm_next / norm_now * direction
            norm_now = norm_next
    scores = accum / math.sqrt(FEATURES)
    return (scores, solution, resid)
```

```python
import math

import jax
import jax.numpy as jnp
from jax import lax
from jax.sharding import PartitionSpec as P

ITERS = 2
DAMPING = 0.1
PLANES, LAYERS, CORES = 4, 8, 2
HALVES, COLUMNS = 2, 4
NEAR = PLANES * CORES
TAIL = 128

X_GROUPS = [[h * COLUMNS + i for i in range(COLUMNS)] for h in range(HALVES)]
SWAP = [(i, (i + COLUMNS) % (HALVES * COLUMNS)) for i in range(HALVES * COLUMNS)]
NEAR_GROUPS = [
    [(y * LAYERS + z) * CORES + c for y in range(PLANES) for c in range(CORES)]
    for z in range(LAYERS)
]
FAR_GROUPS = [
    [(y * LAYERS + z) * CORES + c for z in range(LAYERS)]
    for y in range(PLANES)
    for c in range(CORES)
]


def rounded(x):
    return lax.reduce_precision(x, 8, 7)


def packed(body, scalars):
    high = rounded(scalars)
    middle = rounded(scalars - high)
    low = scalars - high - middle
    tail = jnp.concatenate([high, middle, low], axis=1)
    tail = jnp.pad(tail, [(0, 0), (0, TAIL - tail.shape[1])])
    return jnp.concatenate([body.astype(jnp.bfloat16), tail.astype(jnp.bfloat16)], axis=1)


def unpacked(x, k):
    x = x.astype(jnp.float32)
    body, tail = x[:, :-TAIL], x[:, -TAIL:]
    return body, tail[:, :k] + tail[:, k : 2 * k] + tail[:, 2 * k : 3 * k]


def exchanged(pieces, axis, groups):
    return lax.all_to_all(pieces, axis, 0, 0, tiled=True, axis_index_groups=groups)


def copies(x, n):
    return jnp.broadcast_to(x[None], (n, *x.shape))


def feature_sum(rows, scalars):
    k = scalars.shape[1]
    arrived = exchanged(copies(packed(rows, scalars), COLUMNS), "feat", X_GROUPS)
    body, scal = unpacked(arrived.astype(jnp.float32).sum(axis=0), k)
    mine = packed(body, scal)
    other = lax.ppermute(mine, "feat", SWAP)
    return unpacked(mine.astype(jnp.float32) + other.astype(jnp.float32), k)


def sample_sum(image, scalars):
    k = scalars.shape[1]
    lines = packed(image, scalars)
    pieces = lines.reshape(NEAR, lines.shape[0] // NEAR, lines.shape[1])
    arrived = exchanged(pieces, "samp", NEAR_GROUPS)
    body, scal = unpacked(arrived.astype(jnp.float32).sum(axis=0), k)
    arrived = exchanged(copies(packed(body, scal), LAYERS), "samp", FAR_GROUPS)
    return unpacked(arrived.astype(jnp.float32).sum(axis=0), k)


def gathered(body, scalars):
    k = scalars.shape[1]
    whole = exchanged(copies(packed(body, scalars), NEAR), "samp", NEAR_GROUPS)
    return unpacked(whole.reshape(-1, whole.shape[-1]), k)


def dot(a, b, dims):
    return lax.dot_general(
        a.astype(jnp.bfloat16), b, (dims, ((), ())), preferred_element_type=jnp.float32
    )


def col(x):
    return jnp.sum(x, axis=1, keepdims=True)


def per_device(grads, weights, targets):
    n_samp, n_feat = lax.axis_size("samp"), lax.axis_size("feat")
    total = grads.shape[0] * n_samp
    share = grads.shape[0] // n_feat
    scaled = (weights / total)[None, :]
    me = lax.axis_index("samp")
    near = me // (LAYERS * CORES) * CORES + me % CORES
    lines = targets.shape[1] // NEAR

    def own(x):
        return lax.dynamic_slice_in_dim(x, near * lines, lines, 0)

    base = targets.T
    base_own = own(base)

    rows0, norm0 = feature_sum(dot(base, grads, ((1,), (1,))), col(base * base))
    weighted = rows0 * scaled
    image, curve = sample_sum(dot(weighted, grads, ((1,), (0,))), col(weighted * rows0))
    alpha = own(norm0) / (curve + DAMPING * own(norm0))
    resid_own = base_own - alpha * (image + DAMPING * base_own)
    resid, alpha0 = gathered(resid_own, alpha)

    sums = jnp.concatenate([col(resid * resid), col(resid * base)], axis=1)
    rows1, sums = feature_sum(dot(resid, grads, ((1,), (1,))), sums)
    norm1, cross = sums[:, :1], sums[:, 1:]
    beta = norm1 / norm0
    rows1 = rows1 + beta * rows0
    weighted = rows1 * scaled
    image, curve = sample_sum(dot(weighted, grads, ((1,), (0,))), col(weighted * rows1))
    square = norm1 + 2.0 * beta * cross + beta * beta * norm0
    alpha = own(norm1) / (curve + DAMPING * own(square))
    line_own = resid_own + own(beta) * base_own
    resid_own = resid_own - alpha * (image + DAMPING * line_own)
    last, alpha1 = gathered(resid_own, alpha)

    direction = resid + beta * base
    answer = alpha0 * base + alpha1 * direction
    scores = (alpha0 * rows0 + alpha1 * rows1) / math.sqrt(grads.shape[1] * n_feat)
    scores = lax.dynamic_slice_in_dim(scores.T, lax.axis_index("feat") * share, share, 0)
    return scores, answer.T, last.T


def solution(mesh):
    return jax.shard_map(
        per_device,
        mesh=mesh,
        in_specs=(P("samp", "feat"), P("samp"), P("feat", None)),
        out_specs=(P(("samp", "feat"), None), P("feat", None), P("feat", None)),
        check_vma=False,
    )
```

```python
import functools
import math

import jax
import jax.numpy as jnp
from jax import lax
from jax.experimental import pallas as pl
from jax.experimental.pallas import tpu as pltpu
from jax.sharding import PartitionSpec as P

DAMPING = 0.1
PLANES, LAYERS, CORES = 4, 8, 2
HALVES, COLUMNS = 2, 4
NEAR = PLANES * CORES
TAIL = 128

X_GROUPS = [[h * COLUMNS + i for i in range(COLUMNS)] for h in range(HALVES)]
SWAP = [(i, (i + COLUMNS) % (HALVES * COLUMNS)) for i in range(HALVES * COLUMNS)]
NEAR_GROUPS = [
    [(y * LAYERS + z) * CORES + c for y in range(PLANES) for c in range(CORES)]
    for z in range(LAYERS)
]
FAR_GROUPS = [
    [(y * LAYERS + z) * CORES + c for z in range(LAYERS)]
    for y in range(PLANES)
    for c in range(CORES)
]
F32, BF16 = jnp.float32, jnp.bfloat16


def rounded(x):
    return x.astype(BF16).astype(F32)


def tail_of(*scalars):
    n = scalars[0].shape[0]
    lane = lax.broadcasted_iota(jnp.int32, (n, TAIL), 1)
    tail = jnp.zeros((n, TAIL), F32)
    for i, x in enumerate(scalars):
        x = jnp.broadcast_to(x, (n, TAIL))
        for term in range(3):
            part = rounded(x)
            tail = jnp.where(lane == 3 * i + term, part, tail)
            x = x - part
    return tail


def scalar_in(tail, i):
    lane = lax.broadcasted_iota(jnp.int32, tail.shape, 1)
    return jnp.sum(jnp.where(lane // 3 == i, tail, 0.0), axis=1, keepdims=True)


def wide(x):
    return jnp.broadcast_to(x, (x.shape[0], TAIL))


def dot(a, b, dims):
    return lax.dot_general(a.astype(BF16), b, (dims, ((), ())), preferred_element_type=F32)


def col(x):
    return jnp.sum(x, axis=1, keepdims=True)


def summed(ref):
    x = ref[0].astype(F32)
    for i in range(1, ref.shape[0]):
        x = x + ref[i].astype(F32)
    return x


def put_copies(ref, body, tail):
    m = body.shape[1]
    body, tail = body.astype(BF16), tail.astype(BF16)
    for i in range(ref.shape[0]):
        ref[i, :, :m] = body
        ref[i, :, m:] = tail


def put_pieces(ref, body, tail):
    n, lines, m = ref.shape[0], ref.shape[1], body.shape[1]
    for i in range(n):
        ref[i, :, :m] = body[i * lines : (i + 1) * lines].astype(BF16)
        ref[i, :, m:] = tail[i * lines : (i + 1) * lines].astype(BF16)


def own_lines(ref):
    me = lax.axis_index("samp")
    near = me // (LAYERS * CORES) * CORES + lax.rem(me, CORES)
    lines = ref.shape[0] // NEAR
    return ref[pl.ds(pl.multiple_of(near * lines, lines), lines), :]


def first_rows(grads, base, out):
    b = base[...]
    put_copies(out, dot(b, grads[...], ((1,), (1,))), tail_of(col(b * b)))


def x_total(count, arrived, out):
    m = arrived.shape[2] - TAIL
    total = summed(arrived)
    tail = total[:, m:]
    out[:, :m] = total[:, :m].astype(BF16)
    out[:, m:] = tail_of(*[scalar_in(tail, i) for i in range(count)]).astype(BF16)


def first_image(grads, weights, mine, other, rows, norm, out):
    m = rows.shape[1]
    total = mine[...].astype(F32) + other[...].astype(F32)
    r = total[:, :m]
    rows[...] = r
    norm[...] = wide(scalar_in(total[:, m:], 0))
    weighted = r * weights[...]
    image = dot(weighted, grads[...], ((1,), (0,)))
    put_pieces(out, image, tail_of(col(weighted * r)))


def near_total(arrived, out):
    m = arrived.shape[2] - TAIL
    total = summed(arrived)
    put_copies(out, total[:, :m], tail_of(scalar_in(total[:, m:], 0)))


def first_step(base, norm, arrived, resid, out):
    m = base.shape[1]
    total = summed(arrived)
    b, nn = own_lines(base), own_lines(norm)[:, :1]
    alpha = nn / (scalar_in(total[:, m:], 0) + DAMPING * nn)
    r = b - alpha * (total[:, :m] + DAMPING * b)
    resid[...] = r
    put_copies(out, r, tail_of(alpha))


def lay_out(ref, arrived):
    lines = arrived.shape[1]
    for i in range(arrived.shape[0]):
        ref[i * lines : (i + 1) * lines, :] = arrived[i].astype(F32)


def next_rows(grads, base, arrived, resid, alpha, out, whole):
    m = base.shape[1]
    lay_out(whole, arrived)
    r = whole[:, :m]
    resid[...] = r
    alpha[...] = wide(scalar_in(whole[:, m:], 0))
    put_copies(
        out,
        dot(r, grads[...], ((1,), (1,))),
        tail_of(col(r * r), col(r * base[...])),
    )


def next_image(grads, weights, mine, other, rows0, norm0, rows, norm, square, beta, out):
    m = rows.shape[1]
    total = mine[...].astype(F32) + other[...].astype(F32)
    tail = total[:, m:]
    n0, n1, cross = norm0[:, :1], scalar_in(tail, 0), scalar_in(tail, 1)
    bt = n1 / n0
    r = total[:, :m] + bt * rows0[...]
    rows[...] = r
    norm[...] = wide(n1)
    beta[...] = wide(bt)
    square[...] = wide(n1 + 2.0 * bt * cross + bt * bt * n0)
    weighted = r * weights[...]
    image = dot(weighted, grads[...], ((1,), (0,)))
    put_pieces(out, image, tail_of(col(weighted * r)))


def last_step(base, resid, norm, square, beta, arrived, out):
    m = base.shape[1]
    total = summed(arrived)
    line = resid[...] + own_lines(beta)[:, :1] * own_lines(base)
    alpha = own_lines(norm)[:, :1] / (
        scalar_in(total[:, m:], 0) + DAMPING * own_lines(square)[:, :1]
    )
    r = resid[...] - alpha * (total[:, :m] + DAMPING * line)
    put_copies(out, r, tail_of(alpha))


def outputs(scale, base, resid, beta, alpha0, rows0, rows1, arrived, scores, answer, last, whole):
    m = base.shape[1]
    lay_out(whole, arrived)
    last[...] = whole[:, :m]
    a0, a1 = alpha0[:, :1], scalar_in(whole[:, m:], 0)
    b = base[...]
    answer[...] = a0 * b + a1 * (resid[...] + beta[:, :1] * b)
    every = (a0 * rows0[...] + a1 * rows1[...]) * scale
    share = scores.shape[1]
    feat = lax.axis_index("feat")
    mine = every[:, :share]
    for i in range(1, every.shape[1] // share):
        mine = jnp.where(feat == i, every[:, i * share : (i + 1) * share], mine)
    scores[...] = mine


def call(kernel, outs, *args, scratch=()):
    whole = pl.BlockSpec(memory_space=pltpu.VMEM)
    return pl.pallas_call(
        kernel,
        out_shape=[jax.ShapeDtypeStruct(s, t) for s, t in outs],
        in_specs=[whole] * len(args),
        out_specs=[whole] * len(outs),
        scratch_shapes=list(scratch),
        compiler_params=pltpu.CompilerParams(vmem_limit_bytes=8 * 2**20),
    )(*args)


def exchanged(pieces, axis, groups):
    return lax.all_to_all(pieces, axis, 0, 0, tiled=True, axis_index_groups=groups)


def per_device(grads, weights, targets):
    n_samp, n_feat = lax.axis_size("samp"), lax.axis_size("feat")
    samples = grads.shape[0]
    share = samples // n_feat
    scaled = (weights / (samples * n_samp))[None, :]
    base = targets.T
    dirs, m = base.shape
    lines = dirs // NEAR
    long = m + TAIL
    block, tile = ((dirs, m), F32), ((dirs, TAIL), F32)
    part = ((lines, m), F32)
    to_x = ((COLUMNS, dirs, long), BF16)
    to_half = ((dirs, long), BF16)
    to_near = ((NEAR, lines, long), BF16)
    to_far = ((LAYERS, lines, long), BF16)
    assembled = [pltpu.VMEM((dirs, long), F32)]

    (out,) = call(first_rows, [to_x], grads, base)
    (mine,) = call(functools.partial(x_total, 1), [to_half], exchanged(out, "feat", X_GROUPS))
    other = lax.ppermute(mine, "feat", SWAP)
    rows0, norm0, out = call(
        first_image, [((dirs, samples), F32), tile, to_near], grads, scaled, mine, other
    )
    (out,) = call(near_total, [to_far], exchanged(out, "samp", NEAR_GROUPS))
    resid_own, out = call(
        first_step, [part, to_near], base, norm0, exchanged(out, "samp", FAR_GROUPS)
    )
    resid, alpha0, out = call(
        next_rows,
        [block, tile, to_x],
        grads,
        base,
        exchanged(out, "samp", NEAR_GROUPS),
        scratch=assembled,
    )
    (mine,) = call(functools.partial(x_total, 2), [to_half], exchanged(out, "feat", X_GROUPS))
    other = lax.ppermute(mine, "feat", SWAP)
    rows1, norm1, square, beta, out = call(
        next_image,
        [((dirs, samples), F32), tile, tile, tile, to_near],
        grads,
        scaled,
        mine,
        other,
        rows0,
        norm0,
    )
    (out,) = call(near_total, [to_far], exchanged(out, "samp", NEAR_GROUPS))
    (out,) = call(
        last_step,
        [to_near],
        base,
        resid_own,
        norm1,
        square,
        beta,
        exchanged(out, "samp", FAR_GROUPS),
    )
    scores, answer, last = call(
        functools.partial(outputs, 1.0 / math.sqrt(m * n_feat)),
        [((dirs, share), F32), block, block],
        base,
        resid,
        beta,
        alpha0,
        rows0,
        rows1,
        exchanged(out, "samp", NEAR_GROUPS),
        scratch=assembled,
    )
    return scores.T, answer.T, last.T


def solution(mesh):
    return jax.shard_map(
        per_device,
        mesh=mesh,
        in_specs=(P("samp", "feat"), P("samp"), P("feat", None)),
        out_specs=(P(("samp", "feat"), None), P("feat", None), P("feat", None)),
        check_vma=False,
    )
```

```python
import functools
import math

import jax
import jax.numpy as jnp
from jax import lax
from jax.experimental import pallas as pl
from jax.experimental.pallas import tpu as pltpu
from jax.sharding import PartitionSpec as P

DAMPING = 0.1
PLANES, LAYERS, CORES = 4, 8, 2
HALVES, COLUMNS = 2, 4
NEAR = PLANES * CORES
LINES, LANES = 8, 128
CHUNKS = 4

X_GROUPS = [[h * COLUMNS + i for i in range(COLUMNS)] for h in range(HALVES)]
SWAP = [(i, (i + COLUMNS) % (HALVES * COLUMNS)) for i in range(HALVES * COLUMNS)]
NEAR_GROUPS = [
    [(y * LAYERS + z) * CORES + c for y in range(PLANES) for c in range(CORES)]
    for z in range(LAYERS)
]
FAR_GROUPS = [
    [(y * LAYERS + z) * CORES + c for z in range(LAYERS)]
    for y in range(PLANES)
    for c in range(CORES)
]
F32, BF16 = jnp.float32, jnp.bfloat16


def dot(a, b, dims):
    return lax.dot_general(a.astype(BF16), b, (dims, ((), ())), preferred_element_type=F32)


def col(x):
    return jnp.sum(x, axis=1, keepdims=True)


def iota(shape, axis):
    return lax.broadcasted_iota(jnp.int32, shape, axis)


def as_row(column):
    shape = (column.shape[0], LANES)
    eye = iota(shape, 0) == iota(shape, 1)
    return jnp.sum(jnp.where(eye, jnp.broadcast_to(column, shape), 0.0), axis=0, keepdims=True)


def as_column(row, n, first=0):
    shape = (n, LANES)
    eye = iota(shape, 0) + first == iota(shape, 1)
    return col(jnp.where(eye, jnp.broadcast_to(row, shape), 0.0))


def tail_of(*rows):
    shape = (LINES, LANES)
    tail = jnp.zeros(shape, F32)
    for i, x in enumerate(rows):
        x = jnp.broadcast_to(x, shape)
        for term in range(3):
            part = x.astype(BF16).astype(F32)
            tail = jnp.where(iota(shape, 0) == 3 * i + term, part, tail)
            x = x - part
    return tail


def row_in(tail, i):
    line = iota(tail.shape, 0)
    chosen = (line >= 3 * i) & (line < 3 * i + 3)
    return jnp.sum(jnp.where(chosen, tail, 0.0), axis=0, keepdims=True)


def tiles_of(body):
    return [
        body[i : i + LINES, j : j + LANES]
        for i in range(0, body.shape[0], LINES)
        for j in range(0, body.shape[1], LANES)
    ]


def body_of(tiles, width):
    across = width // LANES
    lines = [
        jnp.concatenate(tiles[i : i + across], axis=1) for i in range(0, len(tiles), across)
    ]
    return jnp.concatenate(lines, axis=0) if len(lines) > 1 else lines[0]


def put(ref, tiles):
    for i, tile in enumerate(tiles):
        ref[i] = tile.astype(BF16)


def put_copies(ref, tiles):
    for i in range(ref.shape[0]):
        put(ref.at[i], tiles)


def tiles_in(ref):
    return [ref[i].astype(F32) for i in range(ref.shape[0])]


def summed(ref):
    totals = tiles_in(ref.at[0])
    for i in range(1, ref.shape[0]):
        totals = [a + b for a, b in zip(totals, tiles_in(ref.at[i]))]
    return totals


def own_first():
    me = lax.axis_index("samp")
    near = me // (LAYERS * CORES) * CORES + lax.rem(me, CORES)
    return near * LINES


def own_lines(ref):
    return ref[pl.ds(pl.multiple_of(own_first(), LINES), LINES), :]


def put_pieces(out, image, curve):
    tiles, tail = tiles_of(image), tail_of(as_row(curve))
    across = len(tiles) // out.shape[0]
    for i in range(out.shape[0]):
        put(out.at[i], tiles[i * across : (i + 1) * across] + [tail])


def first_rows(grads, base, out, held, line, sems):
    high = held.shape[1]
    loads = [pltpu.make_async_copy(base, line, sems.at[CHUNKS])] + [
        pltpu.make_async_copy(grads.at[pl.ds(i * high, high), :], held.at[i], sems.at[i])
        for i in range(CHUNKS)
    ]
    for load in loads:
        load.start()
    loads[0].wait()
    b = line[...]
    tail = tail_of(as_row(col(b * b)))
    packed = b.astype(BF16)
    parts = []
    for i in range(CHUNKS):
        loads[i + 1].wait()
        parts.append(dot(packed, held[i], ((1,), (1,))))
    put_copies(out, tiles_of(jnp.concatenate(parts, axis=1)) + [tail])


def x_total(count, arrived, out):
    tiles = summed(arrived)
    tail = tail_of(*[row_in(tiles[-1], i) for i in range(count)])
    put(out, tiles[:-1] + [tail])


def first_image(grads, weights, mine, other, rows, norm, out):
    tiles = [a + b for a, b in zip(tiles_in(mine), tiles_in(other))]
    r = body_of(tiles[:-1], rows.shape[1])
    rows[...] = r
    norm[...] = row_in(tiles[-1], 0)
    weighted = r * weights[...]
    put_pieces(out, dot(weighted, grads[...], ((1,), (0,))), col(weighted * r))


def near_total(arrived, out):
    tiles = summed(arrived)
    put_copies(out, tiles[:-1] + [tail_of(row_in(tiles[-1], 0))])


def first_step(base, norm, arrived, resid, alpha, out):
    tiles = summed(arrived)
    n = norm[...]
    a = n / (row_in(tiles[-1], 0) + DAMPING * n)
    alpha[...] = a
    b = own_lines(base)
    image = body_of(tiles[:-1], base.shape[1])
    r = b - as_column(a, LINES, own_first()) * (image + DAMPING * b)
    resid[...] = r
    put_copies(out, tiles_of(r))


def laid_out(arrived, width):
    return body_of([t for i in range(arrived.shape[0]) for t in tiles_in(arrived.at[i])], width)


def next_rows(grads, base, arrived, resid, out):
    b = base[...]
    r = laid_out(arrived, b.shape[1])
    resid[...] = r
    tail = tail_of(as_row(col(r * r)), as_row(col(r * b)))
    put_copies(out, tiles_of(dot(r, grads[...], ((1,), (1,)))) + [tail])


def next_image(grads, weights, mine, other, rows0, norm0, rows, norm, square, beta, out):
    tiles = [a + b for a, b in zip(tiles_in(mine), tiles_in(other))]
    n0, n1, cross = norm0[...], row_in(tiles[-1], 0), row_in(tiles[-1], 1)
    bt = n1 / n0
    norm[...] = n1
    beta[...] = bt
    square[...] = n1 + 2.0 * bt * cross + bt * bt * n0
    old = rows0[...]
    r = body_of(tiles[:-1], old.shape[1]) + as_column(bt, old.shape[0]) * old
    rows[...] = r
    weighted = r * weights[...]
    put_pieces(out, dot(weighted, grads[...], ((1,), (0,))), col(weighted * r))


def last_step(base, resid, norm, square, beta, arrived, alpha, out):
    tiles = summed(arrived)
    a = norm[...] / (row_in(tiles[-1], 0) + DAMPING * square[...])
    alpha[...] = a
    first = own_first()
    line = resid[...] + as_column(beta[...], LINES, first) * own_lines(base)
    image = body_of(tiles[:-1], base.shape[1])
    r = resid[...] - as_column(a, LINES, first) * (image + DAMPING * line)
    put_copies(out, tiles_of(r))


def outputs(
    scale, base, resid, beta, alpha0, alpha1, rows0, rows1, arrived, scores, answer, last, *scratch
):
    score_held, answer_held, last_held, sems = scratch
    last_held[...] = laid_out(arrived, base.shape[1])
    stores = [
        pltpu.make_async_copy(held, out, sems.at[i])
        for i, (held, out) in enumerate(
            ((last_held, last), (answer_held, answer), (score_held, scores))
        )
    ]
    stores[0].start()
    b = base[...]
    dirs = b.shape[0]
    a0, a1 = as_column(alpha0[...], dirs), as_column(alpha1[...], dirs)
    answer_held[...] = a0 * b + a1 * (resid[...] + as_column(beta[...], dirs) * b)
    stores[1].start()
    every = (a0 * rows0[...] + a1 * rows1[...]) * scale
    share = scores.shape[0]
    feat = lax.axis_index("feat")
    mine = every[:, :share]
    for i in range(1, every.shape[1] // share):
        mine = jnp.where(feat == i, every[:, i * share : (i + 1) * share], mine)
    score_held[...] = mine.T
    stores[2].start()
    for store in stores:
        store.wait()


VMEM = pl.BlockSpec(memory_space=pltpu.VMEM)
HBM = pl.BlockSpec(memory_space=pltpu.HBM)


def call(kernel, outs, *args, inputs=VMEM, results=VMEM, scratch=()):
    return pl.pallas_call(
        kernel,
        out_shape=[jax.ShapeDtypeStruct(s, t) for s, t in outs],
        in_specs=[inputs] * len(args),
        out_specs=[results] * len(outs),
        scratch_shapes=list(scratch),
        compiler_params=pltpu.CompilerParams(vmem_limit_bytes=8 * 2**20),
    )(*args)


def exchanged(pieces, axis, groups):
    return lax.all_to_all(pieces, axis, 0, 0, tiled=True, axis_index_groups=groups)


def per_device(grads, weights, targets):
    n_samp, n_feat = lax.axis_size("samp"), lax.axis_size("feat")
    samples = grads.shape[0]
    share = samples // n_feat
    scaled = (weights / (samples * n_samp))[None, :]
    base = targets.T
    dirs, m = base.shape
    across = m // LANES
    row_tiles = dirs // LINES * (samples // LANES) + 1
    block, row, part = ((dirs, m), F32), ((1, LANES), F32), ((LINES, m), F32)
    block_rows = ((dirs, samples), F32)
    to_x = ((COLUMNS, row_tiles, LINES, LANES), BF16)
    to_half = ((row_tiles, LINES, LANES), BF16)
    to_near = ((NEAR, across + 1, LINES, LANES), BF16)
    to_far = ((LAYERS, across + 1, LINES, LANES), BF16)
    to_all = ((NEAR, across, LINES, LANES), BF16)

    (out,) = call(
        first_rows,
        [to_x],
        pltpu.with_memory_space_constraint(grads, pltpu.HBM),
        pltpu.with_memory_space_constraint(base, pltpu.HBM),
        inputs=HBM,
        scratch=[
            pltpu.VMEM((CHUNKS, samples // CHUNKS, m), BF16),
            pltpu.VMEM((dirs, m), F32),
            pltpu.SemaphoreType.DMA((CHUNKS + 1,)),
        ],
    )
    (mine,) = call(functools.partial(x_total, 1), [to_half], exchanged(out, "feat", X_GROUPS))
    other = lax.ppermute(mine, "feat", SWAP)
    rows0, norm0, out = call(
        first_image, [block_rows, row, to_near], grads, scaled, mine, other
    )
    (out,) = call(near_total, [to_far], exchanged(out, "samp", NEAR_GROUPS))
    resid_own, alpha0, out = call(
        first_step, [part, row, to_all], base, norm0, exchanged(out, "samp", FAR_GROUPS)
    )
    resid, out = call(
        next_rows, [block, to_x], grads, base, exchanged(out, "samp", NEAR_GROUPS)
    )
    (mine,) = call(functools.partial(x_total, 2), [to_half], exchanged(out, "feat", X_GROUPS))
    other = lax.ppermute(mine, "feat", SWAP)
    rows1, norm1, square, beta, out = call(
        next_image,
        [block_rows, row, row, row, to_near],
        grads,
        scaled,
        mine,
        other,
        rows0,
        norm0,
    )
    (out,) = call(near_total, [to_far], exchanged(out, "samp", NEAR_GROUPS))
    alpha1, out = call(
        last_step,
        [row, to_all],
        base,
        resid_own,
        norm1,
        square,
        beta,
        exchanged(out, "samp", FAR_GROUPS),
    )
    scores, answer, last = call(
        functools.partial(outputs, 1.0 / math.sqrt(m * n_feat)),
        [((share, dirs), F32), block, block],
        base,
        resid,
        beta,
        alpha0,
        alpha1,
        rows0,
        rows1,
        exchanged(out, "samp", NEAR_GROUPS),
        results=HBM,
        scratch=[
            pltpu.VMEM((share, dirs), F32),
            pltpu.VMEM((dirs, m), F32),
            pltpu.VMEM((dirs, m), F32),
            pltpu.SemaphoreType.DMA((3,)),
        ],
    )
    return scores, answer.T, last.T


def solution(mesh):
    return jax.shard_map(
        per_device,
        mesh=mesh,
        in_specs=(P("samp", "feat"), P("samp"), P("feat", None)),
        out_specs=(P(("samp", "feat"), None), P("feat", None), P("feat", None)),
        check_vma=False,
    )
```

```python
import functools
import math

import jax
import jax.numpy as jnp
from jax import lax
from jax.experimental import pallas as pl
from jax.experimental.pallas import tpu as pltpu
from jax.sharding import PartitionSpec as P

DAMPING = 0.1
PLANES, LAYERS, CORES = 4, 8, 2
HALVES, COLUMNS = 2, 4
NEAR = PLANES * CORES
LINES, LANES = 8, 128

X_GROUPS = [[h * COLUMNS + i for i in range(COLUMNS)] for h in range(HALVES)]
SWAP = [(i, (i + COLUMNS) % (HALVES * COLUMNS)) for i in range(HALVES * COLUMNS)]
NEAR_GROUPS = [
    [(y * LAYERS + z) * CORES + c for y in range(PLANES) for c in range(CORES)]
    for z in range(LAYERS)
]
FAR_GROUPS = [
    [(y * LAYERS + z) * CORES + c for z in range(LAYERS)]
    for y in range(PLANES)
    for c in range(CORES)
]
F32, BF16 = jnp.float32, jnp.bfloat16


def dot(a, b, dims):
    return lax.dot_general(a.astype(BF16), b, (dims, ((), ())), preferred_element_type=F32)


def col(x):
    return jnp.sum(x, axis=1, keepdims=True)


def iota(shape, axis):
    return lax.broadcasted_iota(jnp.int32, shape, axis)


def as_row(column):
    shape = (column.shape[0], LANES)
    eye = iota(shape, 0) == iota(shape, 1)
    return jnp.sum(jnp.where(eye, jnp.broadcast_to(column, shape), 0.0), axis=0, keepdims=True)


def as_column(row, n, first=0):
    shape = (n, LANES)
    eye = iota(shape, 0) + first == iota(shape, 1)
    return col(jnp.where(eye, jnp.broadcast_to(row, shape), 0.0))


def tail_of(*rows):
    shape = (LINES, LANES)
    tail = jnp.zeros(shape, F32)
    for i, x in enumerate(rows):
        x = jnp.broadcast_to(x, shape)
        for term in range(3):
            part = x.astype(BF16).astype(F32)
            tail = jnp.where(iota(shape, 0) == 3 * i + term, part, tail)
            x = x - part
    return tail


def row_in(tail, i):
    line = iota(tail.shape, 0)
    chosen = (line >= 3 * i) & (line < 3 * i + 3)
    return jnp.sum(jnp.where(chosen, tail, 0.0), axis=0, keepdims=True)


def column_tail(*columns):
    shape = (columns[0].shape[0], LANES)
    tail = jnp.zeros(shape, F32)
    for i, x in enumerate(columns):
        x = jnp.broadcast_to(x, shape)
        for term in range(3):
            part = x.astype(BF16).astype(F32)
            tail = jnp.where(iota(shape, 1) == 3 * i + term, part, tail)
            x = x - part
    return tail


def column_in(tail, i):
    lane = iota(tail.shape, 1)
    return col(jnp.where((lane >= 3 * i) & (lane < 3 * i + 3), tail, 0.0))


def tiles_of(body):
    return [
        body[i : i + LINES, j : j + LANES]
        for i in range(0, body.shape[0], LINES)
        for j in range(0, body.shape[1], LANES)
    ]


def body_of(tiles, width):
    across = width // LANES
    lines = [
        jnp.concatenate(tiles[i : i + across], axis=1) for i in range(0, len(tiles), across)
    ]
    return jnp.concatenate(lines, axis=0) if len(lines) > 1 else lines[0]


def put(ref, tiles):
    for i, tile in enumerate(tiles):
        ref[i] = tile.astype(BF16)


def put_copies(ref, tiles):
    for i in range(ref.shape[0]):
        put(ref.at[i], tiles)


def tiles_in(ref):
    return [ref[i].astype(F32) for i in range(ref.shape[0])]


def summed(ref):
    totals = tiles_in(ref.at[0])
    for i in range(1, ref.shape[0]):
        totals = [a + b for a, b in zip(totals, tiles_in(ref.at[i]))]
    return totals


def own_first():
    me = lax.axis_index("samp")
    near = me // (LAYERS * CORES) * CORES + lax.rem(me, CORES)
    return near * LINES


def own_lines(ref):
    return ref[pl.ds(pl.multiple_of(own_first(), LINES), LINES), :]


def chosen_part(x, width):
    feat = lax.axis_index("feat")
    mine = x[:, :width]
    for i in range(1, x.shape[1] // width):
        mine = jnp.where(feat == i, x[:, i * width : (i + 1) * width], mine)
    return mine


def first_rows(grads, base, out, held, line, sems):
    loads = [
        pltpu.make_async_copy(base, line, sems.at[0]),
        pltpu.make_async_copy(grads, held, sems.at[1]),
    ]
    for load in loads:
        load.start()
    loads[0].wait()
    b = line[...]
    tail = tail_of(as_row(col(b * b)))
    packed = b.astype(BF16)
    loads[1].wait()
    put_copies(out, tiles_of(dot(packed, held[...], ((1,), (1,)))) + [tail])


def x_total(count, arrived, out):
    tiles = summed(arrived)
    tail = tail_of(*[row_in(tiles[-1], i) for i in range(count)])
    put(out, tiles[:-1] + [tail])


def weight_tiles(weights, curve):
    blocks = [weights[:, i : i + LANES] for i in range(0, weights.shape[1], LANES)]
    shape, n = (LINES, LANES), len(blocks)
    low, high = tail_of(as_row(curve)), jnp.zeros(shape, F32)
    line = iota(shape, 0)
    for i, x in enumerate(blocks):
        x = jnp.broadcast_to(x, shape)
        first = x.astype(BF16).astype(F32)
        second = (x - first).astype(BF16).astype(F32)
        high = jnp.where(line == i, first, jnp.where(line == n + i, second, high))
        low = jnp.where(line == 3 + i, x - first - second, low)
    return [low, high]


def weights_in(low, high, n):
    return jnp.concatenate(
        [high[i : i + 1] + high[n + i : n + i + 1] + low[3 + i : 4 + i] for i in range(n)], axis=1
    )


def first_image(grads, weights, mine, other, rows, norm, out):
    tiles = [a + b for a, b in zip(tiles_in(mine), tiles_in(other))]
    r = body_of(tiles[:-1], rows.shape[1])
    rows[...] = r
    norm[...] = row_in(tiles[-1], 0)
    w = weights[...]
    weighted = r * w
    image = tiles_of(dot(weighted, grads[...], ((1,), (0,))))
    extra = weight_tiles(w, col(weighted * r))
    across = len(image) // out.shape[0]
    for i in range(out.shape[0]):
        put(out.at[i], image[i * across : (i + 1) * across] + extra)


def near_total(arrived, weights, out):
    tiles = summed(arrived)
    put_copies(out, tiles[:-2] + [tail_of(row_in(tiles[-2], 0))])
    low, high = arrived.shape[1] - 2, arrived.shape[1] - 1
    n = len(tiles) - 2
    width = n * LANES
    for i in range(arrived.shape[0]):
        weights[:, i * width : (i + 1) * width] = weights_in(
            arrived[i, low].astype(F32), arrived[i, high].astype(F32), n
        )


def turn(base, norm, arrived, near_grads, resid, image, alpha, curve, out, held, sems):
    high = held.shape[0] // NEAR
    loads = [
        pltpu.make_async_copy(
            near_grads.at[pl.ds(i * high, high), :], held.at[pl.ds(i * high, high), :], sems.at[i]
        )
        for i in range(NEAR)
    ]
    for load in loads:
        load.start()
    tiles = summed(arrived)
    n = norm[...]
    c = row_in(tiles[-1], 0) + DAMPING * n
    a = n / c
    alpha[...] = a
    curve[...] = c
    b = own_lines(base)
    q = body_of(tiles[:-1], base.shape[1]) + DAMPING * b
    r = b - as_column(a, LINES, own_first()) * q
    resid[...] = r
    image[...] = q
    tail = column_tail(col(r * r), col(r * q))
    packed = r.astype(BF16)
    parts = []
    for i in range(NEAR):
        loads[i].wait()
        parts += tiles_of(dot(packed, held[i * high : (i + 1) * high], ((1,), (1,))))
    put_copies(out, parts + [tail])


def x_total_columns(arrived, out):
    tiles = summed(arrived)
    put(out, tiles[:-1] + [column_tail(*[column_in(tiles[-1], i) for i in range(2)])])


def next_image(near_grads, weights, mine, other, rows, sums, out):
    tiles = [a + b for a, b in zip(tiles_in(mine), tiles_in(other))]
    u = body_of(tiles[:-1], rows.shape[1])
    rows[...] = u
    sums[...] = tiles[-1]
    weighted = u * weights[...]
    image = tiles_of(dot(weighted, near_grads[...], ((1,), (0,))))
    put_copies(out, image + [column_tail(col(weighted * u))])


def last_step(norm, curve, resid, image, rows, sums, arrived, out):
    first = own_first()
    tiles = summed(arrived)
    n0, c0 = as_column(norm[...], LINES, first), as_column(curve[...], LINES, first)
    n1, cross = column_in(sums[...], 0), column_in(sums[...], 1)
    beta = n1 / n0
    own = column_in(tiles[-1], 0) + DAMPING * n1
    alpha = n1 / (own + 2.0 * beta * cross + beta * beta * c0)
    r = resid[...]
    q = body_of(tiles[:-1], r.shape[1]) + DAMPING * r + beta * image[...]
    body = tiles_of(r - alpha * q) + tiles_of(r)
    tail = column_tail(alpha, alpha * beta)
    width = r.shape[1]
    share = width // lax.axis_size("feat")
    for i in range(out.shape[0]):
        part = chosen_part(rows[:, i * width : (i + 1) * width], share)
        tile = jnp.concatenate([part, tail[:, : LANES - share]], axis=1)
        put(out.at[i], body + [tile])


def outputs(scale, base, alpha0, rows0, arrived, scores, answer, last, *scratch):
    score_held, answer_held, last_held, sems = scratch
    width, share = base.shape[1], scores.shape[0]
    near, across = arrived.shape[0], width // LANES
    tiles = [tiles_in(arrived.at[i]) for i in range(near)]
    last_held[...] = body_of([t for of in tiles for t in of[:across]], width)
    stores = [
        pltpu.make_async_copy(held, out, sems.at[i])
        for i, (held, out) in enumerate(
            ((last_held, last), (answer_held, answer), (score_held, scores))
        )
    ]
    stores[0].start()
    ends = jnp.concatenate([of[-1] for of in tiles], axis=0)
    u, tail = ends[:, :share], ends[:, share:]
    gain = column_in(tail, 0)
    held = as_column(alpha0[...], base.shape[0]) + column_in(tail, 1)
    resid = body_of([t for of in tiles for t in of[across : 2 * across]], width)
    answer_held[...] = held * base[...] + gain * resid
    stores[1].start()
    mine = held * chosen_part(rows0[...], share) + gain * u
    score_held[...] = (mine * scale).T
    stores[2].start()
    for store in stores:
        store.wait()


VMEM = pl.BlockSpec(memory_space=pltpu.VMEM)
HBM = pl.BlockSpec(memory_space=pltpu.HBM)


def call(kernel, outs, *args, inputs=None, results=VMEM, scratch=()):
    return pl.pallas_call(
        kernel,
        out_shape=[jax.ShapeDtypeStruct(s, t) for s, t in outs],
        in_specs=inputs or [VMEM] * len(args),
        out_specs=[results] * len(outs),
        scratch_shapes=list(scratch),
        compiler_params=pltpu.CompilerParams(vmem_limit_bytes=16 * 2**20),
    )(*args)


def exchanged(pieces, axis, groups):
    return lax.all_to_all(pieces, axis, 0, 0, tiled=True, axis_index_groups=groups)


def per_device(grads, weights, targets):
    n_samp, n_feat = lax.axis_size("samp"), lax.axis_size("feat")
    samples = grads.shape[0]
    share = samples // n_feat
    near_grads = lax.all_gather(grads, "samp", axis_index_groups=NEAR_GROUPS, axis=0, tiled=True)
    scaled = (weights / (samples * n_samp))[None, :]
    base = targets.T
    dirs, m = base.shape
    across = m // LANES
    row_tiles = dirs // LINES * (samples // LANES) + 1
    block, row, part = ((dirs, m), F32), ((1, LANES), F32), ((LINES, m), F32)
    to_x = ((COLUMNS, row_tiles, LINES, LANES), BF16)
    to_half = ((row_tiles, LINES, LANES), BF16)
    to_near = ((NEAR, across + 2, LINES, LANES), BF16)
    to_far = ((LAYERS, across + 1, LINES, LANES), BF16)
    to_all = ((NEAR, 2 * across + 1, LINES, LANES), BF16)

    out, held, base = call(
        first_rows,
        [to_x, (grads.shape, grads.dtype), block],
        pltpu.with_memory_space_constraint(grads, pltpu.HBM),
        pltpu.with_memory_space_constraint(base, pltpu.HBM),
        inputs=[HBM, HBM],
        scratch=[pltpu.SemaphoreType.DMA((2,))],
    )
    (mine,) = call(functools.partial(x_total, 1), [to_half], exchanged(out, "feat", X_GROUPS))
    other = lax.ppermute(mine, "feat", SWAP)
    rows0, norm0, out = call(
        first_image, [((dirs, samples), F32), row, to_near], held, scaled, mine, other
    )
    near_weights, out = call(
        near_total,
        [((1, NEAR * samples), F32), to_far],
        exchanged(out, "samp", NEAR_GROUPS),
    )
    resid, image, alpha0, curve0, out, held = call(
        turn,
        [part, part, row, row, to_x, ((NEAR * samples, m), grads.dtype)],
        base,
        norm0,
        exchanged(out, "samp", FAR_GROUPS),
        pltpu.with_memory_space_constraint(near_grads, pltpu.HBM),
        inputs=[VMEM, VMEM, VMEM, HBM],
        scratch=[pltpu.SemaphoreType.DMA((NEAR,))],
    )
    (mine,) = call(x_total_columns, [to_half], exchanged(out, "feat", X_GROUPS))
    other = lax.ppermute(mine, "feat", SWAP)
    rows1, sums, out = call(
        next_image,
        [((LINES, NEAR * samples), F32), ((LINES, LANES), F32), to_far],
        held,
        near_weights,
        mine,
        other,
    )
    (out,) = call(
        last_step,
        [to_all],
        norm0,
        curve0,
        resid,
        image,
        rows1,
        sums,
        exchanged(out, "samp", FAR_GROUPS),
    )
    scores, answer, last = call(
        functools.partial(outputs, 1.0 / math.sqrt(m * n_feat)),
        [((share, dirs), F32), block, block],
        base,
        alpha0,
        rows0,
        exchanged(out, "samp", NEAR_GROUPS),
        results=HBM,
        scratch=[
            pltpu.VMEM((share, dirs), F32),
            pltpu.VMEM((dirs, m), F32),
            pltpu.VMEM((dirs, m), F32),
            pltpu.SemaphoreType.DMA((3,)),
        ],
    )
    return scores, answer.T, last.T


def solution(mesh):
    return jax.shard_map(
        per_device,
        mesh=mesh,
        in_specs=(P("samp", "feat"), P("samp"), P("feat", None)),
        out_specs=(P(("samp", "feat"), None), P("feat", None), P("feat", None)),
        check_vma=False,
    )
```

```python
import functools
import math

import jax
import jax.numpy as jnp
from jax import lax
from jax.experimental import pallas as pl
from jax.experimental.pallas import tpu as pltpu
from jax.sharding import PartitionSpec as P

DAMPING = 0.1
PLANES, LAYERS, CORES = 4, 8, 2
HALVES, COLUMNS = 2, 4
NEAR = PLANES * CORES
LINES, LANES = 8, 128

X_GROUPS = [[h * COLUMNS + i for i in range(COLUMNS)] for h in range(HALVES)]
SWAP = [(i, (i + COLUMNS) % (HALVES * COLUMNS)) for i in range(HALVES * COLUMNS)]
NEAR_GROUPS = [
    [(y * LAYERS + z) * CORES + c for y in range(PLANES) for c in range(CORES)]
    for z in range(LAYERS)
]
FAR_GROUPS = [
    [(y * LAYERS + z) * CORES + c for z in range(LAYERS)]
    for y in range(PLANES)
    for c in range(CORES)
]
F32, BF16 = jnp.float32, jnp.bfloat16


def dot(a, b, dims):
    return lax.dot_general(a.astype(BF16), b, (dims, ((), ())), preferred_element_type=F32)


def col(x):
    return jnp.sum(x, axis=1, keepdims=True)


def iota(shape, axis):
    return lax.broadcasted_iota(jnp.int32, shape, axis)


def as_row(column):
    shape = (column.shape[0], LANES)
    eye = iota(shape, 0) == iota(shape, 1)
    return jnp.sum(jnp.where(eye, jnp.broadcast_to(column, shape), 0.0), axis=0, keepdims=True)


def as_column(row, n, first=0):
    shape = (n, LANES)
    eye = iota(shape, 0) + first == iota(shape, 1)
    return col(jnp.where(eye, jnp.broadcast_to(row, shape), 0.0))


def tail_of(*rows):
    shape = (LINES, LANES)
    tail = jnp.zeros(shape, F32)
    for i, x in enumerate(rows):
        x = jnp.broadcast_to(x, shape)
        for term in range(3):
            part = x.astype(BF16).astype(F32)
            tail = jnp.where(iota(shape, 0) == 3 * i + term, part, tail)
            x = x - part
    return tail


def row_in(tail, i):
    line = iota(tail.shape, 0)
    chosen = (line >= 3 * i) & (line < 3 * i + 3)
    return jnp.sum(jnp.where(chosen, tail, 0.0), axis=0, keepdims=True)


def tiles_of(body):
    return [
        body[i : i + LINES, j : j + LANES]
        for i in range(0, body.shape[0], LINES)
        for j in range(0, body.shape[1], LANES)
    ]


def body_of(tiles, width):
    across = width // LANES
    lines = [
        jnp.concatenate(tiles[i : i + across], axis=1) for i in range(0, len(tiles), across)
    ]
    return jnp.concatenate(lines, axis=0) if len(lines) > 1 else lines[0]


def put(ref, tiles):
    for i, tile in enumerate(tiles):
        ref[i] = tile.astype(BF16)


def put_copies(ref, tiles):
    for i in range(ref.shape[0]):
        put(ref.at[i], tiles)


def tiles_in(ref):
    return [ref[i].astype(F32) for i in range(ref.shape[0])]


def summed(ref):
    totals = tiles_in(ref.at[0])
    for i in range(1, ref.shape[0]):
        totals = [a + b for a, b in zip(totals, tiles_in(ref.at[i]))]
    return totals


def own_first():
    me = lax.axis_index("samp")
    near = me // (LAYERS * CORES) * CORES + lax.rem(me, CORES)
    return near * LINES


def own_lines(ref):
    return ref[pl.ds(pl.multiple_of(own_first(), LINES), LINES), :]


def put_pieces(out, image, curve):
    tiles, tail = tiles_of(image), tail_of(as_row(curve))
    across = len(tiles) // out.shape[0]
    for i in range(out.shape[0]):
        put(out.at[i], tiles[i * across : (i + 1) * across] + [tail])


def first_rows(grads, base, out, held, line, sems):
    loads = [
        pltpu.make_async_copy(base, line, sems.at[0]),
        pltpu.make_async_copy(grads, held, sems.at[1]),
    ]
    for load in loads:
        load.start()
    loads[0].wait()
    b = line[...]
    tail = tail_of(as_row(col(b * b)))
    packed = b.astype(BF16)
    loads[1].wait()
    put_copies(out, tiles_of(dot(packed, held[...], ((1,), (1,)))) + [tail])


def x_total(count, arrived, out):
    tiles = summed(arrived)
    tail = tail_of(*[row_in(tiles[-1], i) for i in range(count)])
    put(out, tiles[:-1] + [tail])


def first_image(grads, weights, mine, other, rows, norm, out):
    tiles = [a + b for a, b in zip(tiles_in(mine), tiles_in(other))]
    r = body_of(tiles[:-1], rows.shape[1])
    rows[...] = r
    norm[...] = row_in(tiles[-1], 0)
    weighted = r * weights[...]
    put_pieces(out, dot(weighted, grads[...], ((1,), (0,))), col(weighted * r))


def near_total(arrived, out):
    tiles = summed(arrived)
    put_copies(out, tiles[:-1] + [tail_of(row_in(tiles[-1], 0))])


def first_step(base, norm, arrived, resid, alpha, out):
    tiles = summed(arrived)
    n = norm[...]
    a = n / (row_in(tiles[-1], 0) + DAMPING * n)
    alpha[...] = a
    b = own_lines(base)
    image = body_of(tiles[:-1], base.shape[1])
    r = b - as_column(a, LINES, own_first()) * (image + DAMPING * b)
    resid[...] = r
    put_copies(out, tiles_of(r))


def laid_out(arrived, width):
    return body_of([t for i in range(arrived.shape[0]) for t in tiles_in(arrived.at[i])], width)


def next_rows(grads, base, arrived, resid, out):
    b = base[...]
    r = laid_out(arrived, b.shape[1])
    resid[...] = r
    tail = tail_of(as_row(col(r * r)), as_row(col(r * b)))
    put_copies(out, tiles_of(dot(r, grads[...], ((1,), (1,)))) + [tail])


def next_image(grads, weights, mine, other, rows0, norm0, rows, norm, square, beta, out):
    tiles = [a + b for a, b in zip(tiles_in(mine), tiles_in(other))]
    n0, n1, cross = norm0[...], row_in(tiles[-1], 0), row_in(tiles[-1], 1)
    bt = n1 / n0
    norm[...] = n1
    beta[...] = bt
    square[...] = n1 + 2.0 * bt * cross + bt * bt * n0
    old = rows0[...]
    r = body_of(tiles[:-1], old.shape[1]) + as_column(bt, old.shape[0]) * old
    rows[...] = r
    weighted = r * weights[...]
    put_pieces(out, dot(weighted, grads[...], ((1,), (0,))), col(weighted * r))


def last_step(base, resid, norm, square, beta, arrived, alpha, out):
    tiles = summed(arrived)
    a = norm[...] / (row_in(tiles[-1], 0) + DAMPING * square[...])
    alpha[...] = a
    first = own_first()
    line = resid[...] + as_column(beta[...], LINES, first) * own_lines(base)
    image = body_of(tiles[:-1], base.shape[1])
    r = resid[...] - as_column(a, LINES, first) * (image + DAMPING * line)
    put_copies(out, tiles_of(r))


def outputs(
    scale, base, resid, beta, alpha0, alpha1, rows0, rows1, arrived, scores, answer, last, *scratch
):
    score_held, answer_held, last_held, sems = scratch
    last_held[...] = laid_out(arrived, base.shape[1])
    stores = [
        pltpu.make_async_copy(held, out, sems.at[i])
        for i, (held, out) in enumerate(
            ((last_held, last), (answer_held, answer), (score_held, scores))
        )
    ]
    stores[0].start()
    b = base[...]
    dirs = b.shape[0]
    a0, a1 = as_column(alpha0[...], dirs), as_column(alpha1[...], dirs)
    answer_held[...] = a0 * b + a1 * (resid[...] + as_column(beta[...], dirs) * b)
    stores[1].start()
    every = (a0 * rows0[...] + a1 * rows1[...]) * scale
    share = scores.shape[0]
    feat = lax.axis_index("feat")
    mine = every[:, :share]
    for i in range(1, every.shape[1] // share):
        mine = jnp.where(feat == i, every[:, i * share : (i + 1) * share], mine)
    score_held[...] = mine.T
    stores[2].start()
    for store in stores:
        store.wait()


VMEM = pl.BlockSpec(memory_space=pltpu.VMEM)
HBM = pl.BlockSpec(memory_space=pltpu.HBM)


def call(kernel, outs, *args, inputs=VMEM, results=VMEM, scratch=()):
    return pl.pallas_call(
        kernel,
        out_shape=[jax.ShapeDtypeStruct(s, t) for s, t in outs],
        in_specs=[inputs] * len(args),
        out_specs=[results] * len(outs),
        scratch_shapes=list(scratch),
        compiler_params=pltpu.CompilerParams(vmem_limit_bytes=8 * 2**20),
    )(*args)


def exchanged(pieces, axis, groups):
    return lax.all_to_all(pieces, axis, 0, 0, tiled=True, axis_index_groups=groups)


def per_device(grads, weights, targets):
    n_samp, n_feat = lax.axis_size("samp"), lax.axis_size("feat")
    samples = grads.shape[0]
    share = samples // n_feat
    scaled = (weights / (samples * n_samp))[None, :]
    base = targets.T
    dirs, m = base.shape
    across = m // LANES
    row_tiles = dirs // LINES * (samples // LANES) + 1
    block, row, part = ((dirs, m), F32), ((1, LANES), F32), ((LINES, m), F32)
    block_rows = ((dirs, samples), F32)
    to_x = ((COLUMNS, row_tiles, LINES, LANES), BF16)
    to_half = ((row_tiles, LINES, LANES), BF16)
    to_near = ((NEAR, across + 1, LINES, LANES), BF16)
    to_far = ((LAYERS, across + 1, LINES, LANES), BF16)
    to_all = ((NEAR, across, LINES, LANES), BF16)

    out, grads, base = call(
        first_rows,
        [to_x, (grads.shape, grads.dtype), block],
        pltpu.with_memory_space_constraint(grads, pltpu.HBM),
        pltpu.with_memory_space_constraint(base, pltpu.HBM),
        inputs=HBM,
        scratch=[pltpu.SemaphoreType.DMA((2,))],
    )
    (mine,) = call(functools.partial(x_total, 1), [to_half], exchanged(out, "feat", X_GROUPS))
    other = lax.ppermute(mine, "feat", SWAP)
    rows0, norm0, out = call(
        first_image, [block_rows, row, to_near], grads, scaled, mine, other
    )
    (out,) = call(near_total, [to_far], exchanged(out, "samp", NEAR_GROUPS))
    resid_own, alpha0, out = call(
        first_step, [part, row, to_all], base, norm0, exchanged(out, "samp", FAR_GROUPS)
    )
    resid, out = call(
        next_rows, [block, to_x], grads, base, exchanged(out, "samp", NEAR_GROUPS)
    )
    (mine,) = call(functools.partial(x_total, 2), [to_half], exchanged(out, "feat", X_GROUPS))
    other = lax.ppermute(mine, "feat", SWAP)
    rows1, norm1, square, beta, out = call(
        next_image,
        [block_rows, row, row, row, to_near],
        grads,
        scaled,
        mine,
        other,
        rows0,
        norm0,
    )
    (out,) = call(near_total, [to_far], exchanged(out, "samp", NEAR_GROUPS))
    alpha1, out = call(
        last_step,
        [row, to_all],
        base,
        resid_own,
        norm1,
        square,
        beta,
        exchanged(out, "samp", FAR_GROUPS),
    )
    scores, answer, last = call(
        functools.partial(outputs, 1.0 / math.sqrt(m * n_feat)),
        [((share, dirs), F32), block, block],
        base,
        resid,
        beta,
        alpha0,
        alpha1,
        rows0,
        rows1,
        exchanged(out, "samp", NEAR_GROUPS),
        results=HBM,
        scratch=[
            pltpu.VMEM((share, dirs), F32),
            pltpu.VMEM((dirs, m), F32),
            pltpu.VMEM((dirs, m), F32),
            pltpu.SemaphoreType.DMA((3,)),
        ],
    )
    return scores, answer.T, last.T


def solution(mesh):
    return jax.shard_map(
        per_device,
        mesh=mesh,
        in_specs=(P("samp", "feat"), P("samp"), P("feat", None)),
        out_specs=(P(("samp", "feat"), None), P("feat", None), P("feat", None)),
        check_vma=False,
    )
```

```python
import functools
import math

import jax
import jax.numpy as jnp
from jax import lax
from jax.experimental import pallas as pl
from jax.experimental.pallas import tpu as pltpu
from jax.sharding import PartitionSpec as P

DAMPING = 0.1
PLANES, LAYERS, CORES = 4, 8, 2
HALVES, COLUMNS = 2, 4
NEAR = PLANES * CORES
LINES, LANES = 8, 128

X_GROUPS = [[h * COLUMNS + i for i in range(COLUMNS)] for h in range(HALVES)]
SWAP = [(i, (i + COLUMNS) % (HALVES * COLUMNS)) for i in range(HALVES * COLUMNS)]
FAR_ORDER = (3, 7, 0, 6, 1, 5, 2, 4)
NEAR_ORDER = ((0, 1), (0, 0), (1, 0), (3, 1), (2, 1), (2, 0), (1, 1), (3, 0))
NEAR_GROUPS = [[(y * LAYERS + z) * CORES + c for y, c in NEAR_ORDER] for z in range(LAYERS)]
FAR_GROUPS = [
    [(y * LAYERS + z) * CORES + c for z in FAR_ORDER] for y in range(PLANES) for c in range(CORES)
]
F32, BF16 = jnp.float32, jnp.bfloat16


def dot(a, b, dims):
    return lax.dot_general(a.astype(BF16), b, (dims, ((), ())), preferred_element_type=F32)


def col(x):
    return jnp.sum(x, axis=1, keepdims=True)


def iota(shape, axis):
    return lax.broadcasted_iota(jnp.int32, shape, axis)


def as_row(column):
    shape = (column.shape[0], LANES)
    eye = iota(shape, 0) == iota(shape, 1)
    return jnp.sum(jnp.where(eye, jnp.broadcast_to(column, shape), 0.0), axis=0, keepdims=True)


def as_column(row, n, first=0):
    shape = (n, LANES)
    eye = iota(shape, 0) + first == iota(shape, 1)
    return col(jnp.where(eye, jnp.broadcast_to(row, shape), 0.0))


def tail_of(*rows):
    shape = (LINES, LANES)
    tail = jnp.zeros(shape, F32)
    for i, x in enumerate(rows):
        x = jnp.broadcast_to(x, shape)
        for term in range(3):
            part = x.astype(BF16).astype(F32)
            tail = jnp.where(iota(shape, 0) == 3 * i + term, part, tail)
            x = x - part
    return tail


def row_in(tail, i):
    line = iota(tail.shape, 0)
    chosen = (line >= 3 * i) & (line < 3 * i + 3)
    return jnp.sum(jnp.where(chosen, tail, 0.0), axis=0, keepdims=True)


def tiles_of(body):
    return [
        body[i : i + LINES, j : j + LANES]
        for i in range(0, body.shape[0], LINES)
        for j in range(0, body.shape[1], LANES)
    ]


def body_of(tiles, width):
    across = width // LANES
    lines = [
        jnp.concatenate(tiles[i : i + across], axis=1) for i in range(0, len(tiles), across)
    ]
    return jnp.concatenate(lines, axis=0) if len(lines) > 1 else lines[0]


def put(ref, tiles):
    for i, tile in enumerate(tiles):
        ref[i] = tile.astype(BF16)


def put_copies(ref, tiles):
    for i in range(ref.shape[0]):
        put(ref.at[i], tiles)


def tiles_in(ref):
    return [ref[i].astype(F32) for i in range(ref.shape[0])]


def summed(ref):
    totals = tiles_in(ref.at[0])
    for i in range(1, ref.shape[0]):
        totals = [a + b for a, b in zip(totals, tiles_in(ref.at[i]))]
    return totals


def own_first():
    me = lax.axis_index("samp")
    y, c = me // (LAYERS * CORES), lax.rem(me, CORES)
    first = jnp.int32(0)
    for place, (plane, core) in enumerate(NEAR_ORDER):
        first = jnp.where((y == plane) & (c == core), place * LINES, first)
    return first


def own_lines(ref):
    return ref[pl.ds(pl.multiple_of(own_first(), LINES), LINES), :]


def put_pieces(out, image, curve):
    tiles, tail = tiles_of(image), tail_of(as_row(curve))
    across = len(tiles) // out.shape[0]
    for i in range(out.shape[0]):
        put(out.at[i], tiles[i * across : (i + 1) * across] + [tail])


def first_rows(grads, base, out, held, line, sems):
    loads = [
        pltpu.make_async_copy(base, line, sems.at[0]),
        pltpu.make_async_copy(grads, held, sems.at[1]),
    ]
    for load in loads:
        load.start()
    loads[0].wait()
    b = line[...]
    tail = tail_of(as_row(col(b * b)))
    packed = b.astype(BF16)
    loads[1].wait()
    put_copies(out, tiles_of(dot(packed, held[...], ((1,), (1,)))) + [tail])


def x_total(count, arrived, out):
    tiles = summed(arrived)
    tail = tail_of(*[row_in(tiles[-1], i) for i in range(count)])
    put(out, tiles[:-1] + [tail])


def first_image(grads, weights, mine, other, rows, norm, out):
    tiles = [a + b for a, b in zip(tiles_in(mine), tiles_in(other))]
    r = body_of(tiles[:-1], rows.shape[1])
    rows[...] = r
    norm[...] = row_in(tiles[-1], 0)
    weighted = r * weights[...]
    put_pieces(out, dot(weighted, grads[...], ((1,), (0,))), col(weighted * r))


def near_total(arrived, out):
    tiles = summed(arrived)
    put_copies(out, tiles[:-1] + [tail_of(row_in(tiles[-1], 0))])


def first_step(base, norm, arrived, resid, alpha, out):
    tiles = summed(arrived)
    n = norm[...]
    a = n / (row_in(tiles[-1], 0) + DAMPING * n)
    alpha[...] = a
    b = own_lines(base)
    image = body_of(tiles[:-1], base.shape[1])
    r = b - as_column(a, LINES, own_first()) * (image + DAMPING * b)
    resid[...] = r
    put_copies(out, tiles_of(r))


def laid_out(arrived, width):
    return body_of([t for i in range(arrived.shape[0]) for t in tiles_in(arrived.at[i])], width)


def next_rows(grads, base, arrived, resid, out):
    b = base[...]
    r = laid_out(arrived, b.shape[1])
    resid[...] = r
    tail = tail_of(as_row(col(r * r)), as_row(col(r * b)))
    put_copies(out, tiles_of(dot(r, grads[...], ((1,), (1,)))) + [tail])


def next_image(grads, weights, mine, other, rows0, norm0, rows, norm, square, beta, out):
    tiles = [a + b for a, b in zip(tiles_in(mine), tiles_in(other))]
    n0, n1, cross = norm0[...], row_in(tiles[-1], 0), row_in(tiles[-1], 1)
    bt = n1 / n0
    norm[...] = n1
    beta[...] = bt
    square[...] = n1 + 2.0 * bt * cross + bt * bt * n0
    old = rows0[...]
    r = body_of(tiles[:-1], old.shape[1]) + as_column(bt, old.shape[0]) * old
    rows[...] = r
    weighted = r * weights[...]
    put_pieces(out, dot(weighted, grads[...], ((1,), (0,))), col(weighted * r))


def last_step(base, resid, norm, square, beta, arrived, alpha, out):
    tiles = summed(arrived)
    a = norm[...] / (row_in(tiles[-1], 0) + DAMPING * square[...])
    alpha[...] = a
    first = own_first()
    line = resid[...] + as_column(beta[...], LINES, first) * own_lines(base)
    image = body_of(tiles[:-1], base.shape[1])
    r = resid[...] - as_column(a, LINES, first) * (image + DAMPING * line)
    put_copies(out, tiles_of(r))


def outputs(
    scale, base, resid, beta, alpha0, alpha1, rows0, rows1, arrived, scores, answer, last, *scratch
):
    score_held, answer_held, last_held, sems = scratch
    last_held[...] = laid_out(arrived, base.shape[1])
    stores = [
        pltpu.make_async_copy(held, out, sems.at[i])
        for i, (held, out) in enumerate(
            ((last_held, last), (answer_held, answer), (score_held, scores))
        )
    ]
    stores[0].start()
    b = base[...]
    dirs = b.shape[0]
    a0, a1 = as_column(alpha0[...], dirs), as_column(alpha1[...], dirs)
    answer_held[...] = a0 * b + a1 * (resid[...] + as_column(beta[...], dirs) * b)
    stores[1].start()
    every = (a0 * rows0[...] + a1 * rows1[...]) * scale
    share = scores.shape[0]
    feat = lax.axis_index("feat")
    mine = every[:, :share]
    for i in range(1, every.shape[1] // share):
        mine = jnp.where(feat == i, every[:, i * share : (i + 1) * share], mine)
    score_held[...] = mine.T
    stores[2].start()
    for store in stores:
        store.wait()


VMEM = pl.BlockSpec(memory_space=pltpu.VMEM)
HBM = pl.BlockSpec(memory_space=pltpu.HBM)


def call(kernel, outs, *args, inputs=VMEM, results=VMEM, scratch=()):
    return pl.pallas_call(
        kernel,
        out_shape=[jax.ShapeDtypeStruct(s, t) for s, t in outs],
        in_specs=[inputs] * len(args),
        out_specs=[results] * len(outs),
        scratch_shapes=list(scratch),
        compiler_params=pltpu.CompilerParams(vmem_limit_bytes=8 * 2**20),
    )(*args)


def exchanged(pieces, axis, groups):
    return lax.all_to_all(pieces, axis, 0, 0, tiled=True, axis_index_groups=groups)


def per_device(grads, weights, targets):
    n_samp, n_feat = lax.axis_size("samp"), lax.axis_size("feat")
    samples = grads.shape[0]
    share = samples // n_feat
    scaled = (weights / (samples * n_samp))[None, :]
    base = targets.T
    dirs, m = base.shape
    across = m // LANES
    row_tiles = dirs // LINES * (samples // LANES) + 1
    block, row, part = ((dirs, m), F32), ((1, LANES), F32), ((LINES, m), F32)
    block_rows = ((dirs, samples), F32)
    to_x = ((COLUMNS, row_tiles, LINES, LANES), BF16)
    to_half = ((row_tiles, LINES, LANES), BF16)
    to_near = ((NEAR, across + 1, LINES, LANES), BF16)
    to_far = ((LAYERS, across + 1, LINES, LANES), BF16)
    to_all = ((NEAR, across, LINES, LANES), BF16)

    out, grads, base = call(
        first_rows,
        [to_x, (grads.shape, grads.dtype), block],
        pltpu.with_memory_space_constraint(grads, pltpu.HBM),
        pltpu.with_memory_space_constraint(base, pltpu.HBM),
        inputs=HBM,
        scratch=[pltpu.SemaphoreType.DMA((2,))],
    )
    (mine,) = call(functools.partial(x_total, 1), [to_half], exchanged(out, "feat", X_GROUPS))
    other = lax.ppermute(mine, "feat", SWAP)
    rows0, norm0, out = call(
        first_image, [block_rows, row, to_near], grads, scaled, mine, other
    )
    (out,) = call(near_total, [to_far], exchanged(out, "samp", NEAR_GROUPS))
    resid_own, alpha0, out = call(
        first_step, [part, row, to_all], base, norm0, exchanged(out, "samp", FAR_GROUPS)
    )
    resid, out = call(
        next_rows, [block, to_x], grads, base, exchanged(out, "samp", NEAR_GROUPS)
    )
    (mine,) = call(functools.partial(x_total, 2), [to_half], exchanged(out, "feat", X_GROUPS))
    other = lax.ppermute(mine, "feat", SWAP)
    rows1, norm1, square, beta, out = call(
        next_image,
        [block_rows, row, row, row, to_near],
        grads,
        scaled,
        mine,
        other,
        rows0,
        norm0,
    )
    (out,) = call(near_total, [to_far], exchanged(out, "samp", NEAR_GROUPS))
    alpha1, out = call(
        last_step,
        [row, to_all],
        base,
        resid_own,
        norm1,
        square,
        beta,
        exchanged(out, "samp", FAR_GROUPS),
    )
    scores, answer, last = call(
        functools.partial(outputs, 1.0 / math.sqrt(m * n_feat)),
        [((share, dirs), F32), block, block],
        base,
        resid,
        beta,
        alpha0,
        alpha1,
        rows0,
        rows1,
        exchanged(out, "samp", NEAR_GROUPS),
        results=HBM,
        scratch=[
            pltpu.VMEM((share, dirs), F32),
            pltpu.VMEM((dirs, m), F32),
            pltpu.VMEM((dirs, m), F32),
            pltpu.SemaphoreType.DMA((3,)),
        ],
    )
    return scores, answer.T, last.T


def solution(mesh):
    return jax.shard_map(
        per_device,
        mesh=mesh,
        in_specs=(P("samp", "feat"), P("samp"), P("feat", None)),
        out_specs=(P(("samp", "feat"), None), P("feat", None), P("feat", None)),
        check_vma=False,
    )
```

```python
import functools
import math

import jax
import jax.numpy as jnp
from jax import lax
from jax.experimental import pallas as pl
from jax.experimental.pallas import tpu as pltpu
from jax.sharding import PartitionSpec as P

DAMPING = 0.1
PLANES, LAYERS, CORES = 4, 8, 2
HALVES, COLUMNS = 2, 4
NEAR = PLANES * CORES
LINES, LANES = 8, 128

X_GROUPS = [[h * COLUMNS + i for i in range(COLUMNS)] for h in range(HALVES)]
SWAP = [(i, (i + COLUMNS) % (HALVES * COLUMNS)) for i in range(HALVES * COLUMNS)]
FAR_ORDER = (3, 7, 0, 6, 1, 5, 2, 4)
NEAR_ORDER = ((0, 1), (1, 0), (2, 1), (3, 0), (0, 0), (1, 1), (2, 0), (3, 1))
NEAR_GROUPS = [[(y * LAYERS + z) * CORES + c for y, c in NEAR_ORDER] for z in range(LAYERS)]
FAR_GROUPS = [
    [(y * LAYERS + z) * CORES + c for z in FAR_ORDER] for y in range(PLANES) for c in range(CORES)
]
F32, BF16 = jnp.float32, jnp.bfloat16


def dot(a, b, dims):
    return lax.dot_general(a.astype(BF16), b, (dims, ((), ())), preferred_element_type=F32)


def col(x):
    return jnp.sum(x, axis=1, keepdims=True)


def iota(shape, axis):
    return lax.broadcasted_iota(jnp.int32, shape, axis)


def as_row(column):
    shape = (column.shape[0], LANES)
    eye = iota(shape, 0) == iota(shape, 1)
    return jnp.sum(jnp.where(eye, jnp.broadcast_to(column, shape), 0.0), axis=0, keepdims=True)


def as_column(row, n, first=0):
    shape = (n, LANES)
    eye = iota(shape, 0) + first == iota(shape, 1)
    return col(jnp.where(eye, jnp.broadcast_to(row, shape), 0.0))


def tail_of(*rows):
    shape = (LINES, LANES)
    tail = jnp.zeros(shape, F32)
    for i, x in enumerate(rows):
        x = jnp.broadcast_to(x, shape)
        for term in range(3):
            part = x.astype(BF16).astype(F32)
            tail = jnp.where(iota(shape, 0) == 3 * i + term, part, tail)
            x = x - part
    return tail


def row_in(tail, i):
    line = iota(tail.shape, 0)
    chosen = (line >= 3 * i) & (line < 3 * i + 3)
    return jnp.sum(jnp.where(chosen, tail, 0.0), axis=0, keepdims=True)


def tiles_of(body):
    return [
        body[i : i + LINES, j : j + LANES]
        for i in range(0, body.shape[0], LINES)
        for j in range(0, body.shape[1], LANES)
    ]


def body_of(tiles, width):
    across = width // LANES
    lines = [
        jnp.concatenate(tiles[i : i + across], axis=1) for i in range(0, len(tiles), across)
    ]
    return jnp.concatenate(lines, axis=0) if len(lines) > 1 else lines[0]


def put(ref, tiles):
    for i, tile in enumerate(tiles):
        ref[i] = tile.astype(BF16)


def put_copies(ref, tiles):
    for i in range(ref.shape[0]):
        put(ref.at[i], tiles)


def tiles_in(ref):
    return [ref[i].astype(F32) for i in range(ref.shape[0])]


def summed(ref):
    totals = tiles_in(ref.at[0])
    for i in range(1, ref.shape[0]):
        totals = [a + b for a, b in zip(totals, tiles_in(ref.at[i]))]
    return totals


def own_first():
    me = lax.axis_index("samp")
    y, c = me // (LAYERS * CORES), lax.rem(me, CORES)
    first = jnp.int32(0)
    for place, (plane, core) in enumerate(NEAR_ORDER):
        first = jnp.where((y == plane) & (c == core), place * LINES, first)
    return first


def own_lines(ref):
    return ref[pl.ds(pl.multiple_of(own_first(), LINES), LINES), :]


def put_pieces(out, image, curve):
    tiles, tail = tiles_of(image), tail_of(as_row(curve))
    across = len(tiles) // out.shape[0]
    for i in range(out.shape[0]):
        put(out.at[i], tiles[i * across : (i + 1) * across] + [tail])


def first_rows(grads, base, out, held, line, sems):
    loads = [
        pltpu.make_async_copy(base, line, sems.at[0]),
        pltpu.make_async_copy(grads, held, sems.at[1]),
    ]
    for load in loads:
        load.start()
    loads[0].wait()
    b = line[...]
    tail = tail_of(as_row(col(b * b)))
    packed = b.astype(BF16)
    loads[1].wait()
    put_copies(out, tiles_of(dot(packed, held[...], ((1,), (1,)))) + [tail])


def x_total(count, arrived, out):
    tiles = summed(arrived)
    tail = tail_of(*[row_in(tiles[-1], i) for i in range(count)])
    put(out, tiles[:-1] + [tail])


def first_image(grads, weights, mine, other, rows, norm, out):
    tiles = [a + b for a, b in zip(tiles_in(mine), tiles_in(other))]
    r = body_of(tiles[:-1], rows.shape[1])
    rows[...] = r
    norm[...] = row_in(tiles[-1], 0)
    weighted = r * weights[...]
    put_pieces(out, dot(weighted, grads[...], ((1,), (0,))), col(weighted * r))


def near_total(arrived, out):
    tiles = summed(arrived)
    put_copies(out, tiles[:-1] + [tail_of(row_in(tiles[-1], 0))])


def first_step(base, norm, arrived, resid, alpha, out):
    tiles = summed(arrived)
    n = norm[...]
    a = n / (row_in(tiles[-1], 0) + DAMPING * n)
    alpha[...] = a
    b = own_lines(base)
    image = body_of(tiles[:-1], base.shape[1])
    r = b - as_column(a, LINES, own_first()) * (image + DAMPING * b)
    resid[...] = r
    put_copies(out, tiles_of(r))


def laid_out(arrived, width):
    return body_of([t for i in range(arrived.shape[0]) for t in tiles_in(arrived.at[i])], width)


def next_rows(grads, base, arrived, resid, out):
    b = base[...]
    r = laid_out(arrived, b.shape[1])
    resid[...] = r
    tail = tail_of(as_row(col(r * r)), as_row(col(r * b)))
    put_copies(out, tiles_of(dot(r, grads[...], ((1,), (1,)))) + [tail])


def next_image(grads, weights, mine, other, rows0, norm0, rows, norm, square, beta, out):
    tiles = [a + b for a, b in zip(tiles_in(mine), tiles_in(other))]
    n0, n1, cross = norm0[...], row_in(tiles[-1], 0), row_in(tiles[-1], 1)
    bt = n1 / n0
    norm[...] = n1
    beta[...] = bt
    square[...] = n1 + 2.0 * bt * cross + bt * bt * n0
    old = rows0[...]
    r = body_of(tiles[:-1], old.shape[1]) + as_column(bt, old.shape[0]) * old
    rows[...] = r
    weighted = r * weights[...]
    put_pieces(out, dot(weighted, grads[...], ((1,), (0,))), col(weighted * r))


def last_step(base, resid, norm, square, beta, arrived, alpha, out):
    tiles = summed(arrived)
    a = norm[...] / (row_in(tiles[-1], 0) + DAMPING * square[...])
    alpha[...] = a
    first = own_first()
    line = resid[...] + as_column(beta[...], LINES, first) * own_lines(base)
    image = body_of(tiles[:-1], base.shape[1])
    r = resid[...] - as_column(a, LINES, first) * (image + DAMPING * line)
    put_copies(out, tiles_of(r))


def outputs(
    scale, base, resid, beta, alpha0, alpha1, rows0, rows1, arrived, scores, answer, last, *scratch
):
    score_held, answer_held, last_held, sems = scratch
    last_held[...] = laid_out(arrived, base.shape[1])
    stores = [
        pltpu.make_async_copy(held, out, sems.at[i])
        for i, (held, out) in enumerate(
            ((last_held, last), (answer_held, answer), (score_held, scores))
        )
    ]
    stores[0].start()
    b = base[...]
    dirs = b.shape[0]
    a0, a1 = as_column(alpha0[...], dirs), as_column(alpha1[...], dirs)
    answer_held[...] = a0 * b + a1 * (resid[...] + as_column(beta[...], dirs) * b)
    stores[1].start()
    every = (a0 * rows0[...] + a1 * rows1[...]) * scale
    share = scores.shape[0]
    feat = lax.axis_index("feat")
    mine = every[:, :share]
    for i in range(1, every.shape[1] // share):
        mine = jnp.where(feat == i, every[:, i * share : (i + 1) * share], mine)
    score_held[...] = mine.T
    stores[2].start()
    for store in stores:
        store.wait()


VMEM = pl.BlockSpec(memory_space=pltpu.VMEM)
HBM = pl.BlockSpec(memory_space=pltpu.HBM)


def call(kernel, outs, *args, inputs=VMEM, results=VMEM, scratch=()):
    return pl.pallas_call(
        kernel,
        out_shape=[jax.ShapeDtypeStruct(s, t) for s, t in outs],
        in_specs=[inputs] * len(args),
        out_specs=[results] * len(outs),
        scratch_shapes=list(scratch),
        compiler_params=pltpu.CompilerParams(vmem_limit_bytes=8 * 2**20),
    )(*args)


def exchanged(pieces, axis, groups):
    return lax.all_to_all(pieces, axis, 0, 0, tiled=True, axis_index_groups=groups)


def per_device(grads, weights, targets):
    n_samp, n_feat = lax.axis_size("samp"), lax.axis_size("feat")
    samples = grads.shape[0]
    share = samples // n_feat
    scaled = (weights / (samples * n_samp))[None, :]
    base = targets.T
    dirs, m = base.shape
    across = m // LANES
    row_tiles = dirs // LINES * (samples // LANES) + 1
    block, row, part = ((dirs, m), F32), ((1, LANES), F32), ((LINES, m), F32)
    block_rows = ((dirs, samples), F32)
    to_x = ((COLUMNS, row_tiles, LINES, LANES), BF16)
    to_half = ((row_tiles, LINES, LANES), BF16)
    to_near = ((NEAR, across + 1, LINES, LANES), BF16)
    to_far = ((LAYERS, across + 1, LINES, LANES), BF16)
    to_all = ((NEAR, across, LINES, LANES), BF16)

    out, grads, base = call(
        first_rows,
        [to_x, (grads.shape, grads.dtype), block],
        pltpu.with_memory_space_constraint(grads, pltpu.HBM),
        pltpu.with_memory_space_constraint(base, pltpu.HBM),
        inputs=HBM,
        scratch=[pltpu.SemaphoreType.DMA((2,))],
    )
    (mine,) = call(functools.partial(x_total, 1), [to_half], exchanged(out, "feat", X_GROUPS))
    other = lax.ppermute(mine, "feat", SWAP)
    rows0, norm0, out = call(
        first_image, [block_rows, row, to_near], grads, scaled, mine, other
    )
    (out,) = call(near_total, [to_far], exchanged(out, "samp", NEAR_GROUPS))
    resid_own, alpha0, out = call(
        first_step, [part, row, to_all], base, norm0, exchanged(out, "samp", FAR_GROUPS)
    )
    resid, out = call(
        next_rows, [block, to_x], grads, base, exchanged(out, "samp", NEAR_GROUPS)
    )
    (mine,) = call(functools.partial(x_total, 2), [to_half], exchanged(out, "feat", X_GROUPS))
    other = lax.ppermute(mine, "feat", SWAP)
    rows1, norm1, square, beta, out = call(
        next_image,
        [block_rows, row, row, row, to_near],
        grads,
        scaled,
        mine,
        other,
        rows0,
        norm0,
    )
    (out,) = call(near_total, [to_far], exchanged(out, "samp", NEAR_GROUPS))
    alpha1, out = call(
        last_step,
        [row, to_all],
        base,
        resid_own,
        norm1,
        square,
        beta,
        exchanged(out, "samp", FAR_GROUPS),
    )
    scores, answer, last = call(
        functools.partial(outputs, 1.0 / math.sqrt(m * n_feat)),
        [((share, dirs), F32), block, block],
        base,
        resid,
        beta,
        alpha0,
        alpha1,
        rows0,
        rows1,
        exchanged(out, "samp", NEAR_GROUPS),
        results=HBM,
        scratch=[
            pltpu.VMEM((share, dirs), F32),
            pltpu.VMEM((dirs, m), F32),
            pltpu.VMEM((dirs, m), F32),
            pltpu.SemaphoreType.DMA((3,)),
        ],
    )
    return scores, answer.T, last.T


def solution(mesh):
    return jax.shard_map(
        per_device,
        mesh=mesh,
        in_specs=(P("samp", "feat"), P("samp"), P("feat", None)),
        out_specs=(P(("samp", "feat"), None), P("feat", None), P("feat", None)),
        check_vma=False,
    )
```

```python
import functools
import math

import jax
import jax.numpy as jnp
from jax import lax
from jax.experimental import pallas as pl
from jax.experimental.pallas import tpu as pltpu
from jax.sharding import PartitionSpec as P

DAMPING = 0.1
PLANES, LAYERS, CORES = 4, 8, 2
HALVES, COLUMNS = 2, 4
NEAR = PLANES * CORES
LINES, LANES = 8, 128

X_GROUPS = [[h * COLUMNS + i for i in range(COLUMNS)] for h in range(HALVES)]
SWAP = [(i, (i + COLUMNS) % (HALVES * COLUMNS)) for i in range(HALVES * COLUMNS)]
FAR_ORDER = (3, 7, 0, 6, 1, 5, 2, 4)
NEAR_ORDER = ((0, 1), (0, 0), (1, 1), (1, 0), (2, 1), (2, 0), (3, 1), (3, 0))
NEAR_GROUPS = [[(y * LAYERS + z) * CORES + c for y, c in NEAR_ORDER] for z in range(LAYERS)]
FAR_GROUPS = [
    [(y * LAYERS + z) * CORES + c for z in FAR_ORDER] for y in range(PLANES) for c in range(CORES)
]
F32, BF16 = jnp.float32, jnp.bfloat16


def dot(a, b, dims):
    return lax.dot_general(a.astype(BF16), b, (dims, ((), ())), preferred_element_type=F32)


def col(x):
    return jnp.sum(x, axis=1, keepdims=True)


def iota(shape, axis):
    return lax.broadcasted_iota(jnp.int32, shape, axis)


def as_row(column):
    shape = (column.shape[0], LANES)
    eye = iota(shape, 0) == iota(shape, 1)
    return jnp.sum(jnp.where(eye, jnp.broadcast_to(column, shape), 0.0), axis=0, keepdims=True)


def as_column(row, n, first=0):
    shape = (n, LANES)
    eye = iota(shape, 0) + first == iota(shape, 1)
    return col(jnp.where(eye, jnp.broadcast_to(row, shape), 0.0))


def tail_of(*rows):
    shape = (LINES, LANES)
    tail = jnp.zeros(shape, F32)
    for i, x in enumerate(rows):
        x = jnp.broadcast_to(x, shape)
        for term in range(3):
            part = x.astype(BF16).astype(F32)
            tail = jnp.where(iota(shape, 0) == 3 * i + term, part, tail)
            x = x - part
    return tail


def row_in(tail, i):
    line = iota(tail.shape, 0)
    chosen = (line >= 3 * i) & (line < 3 * i + 3)
    return jnp.sum(jnp.where(chosen, tail, 0.0), axis=0, keepdims=True)


def tiles_of(body):
    return [
        body[i : i + LINES, j : j + LANES]
        for i in range(0, body.shape[0], LINES)
        for j in range(0, body.shape[1], LANES)
    ]


def body_of(tiles, width):
    across = width // LANES
    lines = [
        jnp.concatenate(tiles[i : i + across], axis=1) for i in range(0, len(tiles), across)
    ]
    return jnp.concatenate(lines, axis=0) if len(lines) > 1 else lines[0]


def put(ref, tiles):
    for i, tile in enumerate(tiles):
        ref[i] = tile.astype(BF16)


def put_copies(ref, tiles):
    for i in range(ref.shape[0]):
        put(ref.at[i], tiles)


def tiles_in(ref):
    return [ref[i].astype(F32) for i in range(ref.shape[0])]


def summed(ref):
    totals = tiles_in(ref.at[0])
    for i in range(1, ref.shape[0]):
        totals = [a + b for a, b in zip(totals, tiles_in(ref.at[i]))]
    return totals


def own_first():
    me = lax.axis_index("samp")
    y, c = me // (LAYERS * CORES), lax.rem(me, CORES)
    first = jnp.int32(0)
    for place, (plane, core) in enumerate(NEAR_ORDER):
        first = jnp.where((y == plane) & (c == core), place * LINES, first)
    return first


def own_lines(ref):
    return ref[pl.ds(pl.multiple_of(own_first(), LINES), LINES), :]


def put_pieces(out, image, curve):
    tiles, tail = tiles_of(image), tail_of(as_row(curve))
    across = len(tiles) // out.shape[0]
    for i in range(out.shape[0]):
        put(out.at[i], tiles[i * across : (i + 1) * across] + [tail])


def first_rows(grads, base, out, held, line, sems):
    loads = [
        pltpu.make_async_copy(base, line, sems.at[0]),
        pltpu.make_async_copy(grads, held, sems.at[1]),
    ]
    for load in loads:
        load.start()
    loads[0].wait()
    b = line[...]
    tail = tail_of(as_row(col(b * b)))
    packed = b.astype(BF16)
    loads[1].wait()
    put_copies(out, tiles_of(dot(packed, held[...], ((1,), (1,)))) + [tail])


def x_total(count, arrived, out):
    tiles = summed(arrived)
    tail = tail_of(*[row_in(tiles[-1], i) for i in range(count)])
    put(out, tiles[:-1] + [tail])


def first_image(grads, weights, mine, other, rows, norm, out):
    tiles = [a + b for a, b in zip(tiles_in(mine), tiles_in(other))]
    r = body_of(tiles[:-1], rows.shape[1])
    rows[...] = r
    norm[...] = row_in(tiles[-1], 0)
    weighted = r * weights[...]
    put_pieces(out, dot(weighted, grads[...], ((1,), (0,))), col(weighted * r))


def near_total(arrived, out):
    tiles = summed(arrived)
    put_copies(out, tiles[:-1] + [tail_of(row_in(tiles[-1], 0))])


def first_step(base, norm, arrived, resid, alpha, out):
    tiles = summed(arrived)
    n = norm[...]
    a = n / (row_in(tiles[-1], 0) + DAMPING * n)
    alpha[...] = a
    b = own_lines(base)
    image = body_of(tiles[:-1], base.shape[1])
    r = b - as_column(a, LINES, own_first()) * (image + DAMPING * b)
    resid[...] = r
    put_copies(out, tiles_of(r))


def laid_out(arrived, width):
    return body_of([t for i in range(arrived.shape[0]) for t in tiles_in(arrived.at[i])], width)


def next_rows(grads, base, arrived, resid, out):
    b = base[...]
    r = laid_out(arrived, b.shape[1])
    resid[...] = r
    tail = tail_of(as_row(col(r * r)), as_row(col(r * b)))
    put_copies(out, tiles_of(dot(r, grads[...], ((1,), (1,)))) + [tail])


def next_image(grads, weights, mine, other, rows0, norm0, rows, norm, square, beta, out):
    tiles = [a + b for a, b in zip(tiles_in(mine), tiles_in(other))]
    n0, n1, cross = norm0[...], row_in(tiles[-1], 0), row_in(tiles[-1], 1)
    bt = n1 / n0
    norm[...] = n1
    beta[...] = bt
    square[...] = n1 + 2.0 * bt * cross + bt * bt * n0
    old = rows0[...]
    r = body_of(tiles[:-1], old.shape[1]) + as_column(bt, old.shape[0]) * old
    rows[...] = r
    weighted = r * weights[...]
    put_pieces(out, dot(weighted, grads[...], ((1,), (0,))), col(weighted * r))


def last_step(base, resid, norm, square, beta, arrived, alpha, out):
    tiles = summed(arrived)
    a = norm[...] / (row_in(tiles[-1], 0) + DAMPING * square[...])
    alpha[...] = a
    first = own_first()
    line = resid[...] + as_column(beta[...], LINES, first) * own_lines(base)
    image = body_of(tiles[:-1], base.shape[1])
    r = resid[...] - as_column(a, LINES, first) * (image + DAMPING * line)
    put_copies(out, tiles_of(r))


def outputs(
    scale, base, resid, beta, alpha0, alpha1, rows0, rows1, arrived, scores, answer, last, *scratch
):
    score_held, answer_held, last_held, sems = scratch
    last_held[...] = laid_out(arrived, base.shape[1])
    stores = [
        pltpu.make_async_copy(held, out, sems.at[i])
        for i, (held, out) in enumerate(
            ((last_held, last), (answer_held, answer), (score_held, scores))
        )
    ]
    stores[0].start()
    b = base[...]
    dirs = b.shape[0]
    a0, a1 = as_column(alpha0[...], dirs), as_column(alpha1[...], dirs)
    answer_held[...] = a0 * b + a1 * (resid[...] + as_column(beta[...], dirs) * b)
    stores[1].start()
    every = (a0 * rows0[...] + a1 * rows1[...]) * scale
    share = scores.shape[0]
    feat = lax.axis_index("feat")
    mine = every[:, :share]
    for i in range(1, every.shape[1] // share):
        mine = jnp.where(feat == i, every[:, i * share : (i + 1) * share], mine)
    score_held[...] = mine.T
    stores[2].start()
    for store in stores:
        store.wait()


VMEM = pl.BlockSpec(memory_space=pltpu.VMEM)
HBM = pl.BlockSpec(memory_space=pltpu.HBM)


def call(kernel, outs, *args, inputs=VMEM, results=VMEM, scratch=()):
    return pl.pallas_call(
        kernel,
        out_shape=[jax.ShapeDtypeStruct(s, t) for s, t in outs],
        in_specs=[inputs] * len(args),
        out_specs=[results] * len(outs),
        scratch_shapes=list(scratch),
        compiler_params=pltpu.CompilerParams(vmem_limit_bytes=8 * 2**20),
    )(*args)


def exchanged(pieces, axis, groups):
    return lax.all_to_all(pieces, axis, 0, 0, tiled=True, axis_index_groups=groups)


def per_device(grads, weights, targets):
    n_samp, n_feat = lax.axis_size("samp"), lax.axis_size("feat")
    samples = grads.shape[0]
    share = samples // n_feat
    scaled = (weights / (samples * n_samp))[None, :]
    base = targets.T
    dirs, m = base.shape
    across = m // LANES
    row_tiles = dirs // LINES * (samples // LANES) + 1
    block, row, part = ((dirs, m), F32), ((1, LANES), F32), ((LINES, m), F32)
    block_rows = ((dirs, samples), F32)
    to_x = ((COLUMNS, row_tiles, LINES, LANES), BF16)
    to_half = ((row_tiles, LINES, LANES), BF16)
    to_near = ((NEAR, across + 1, LINES, LANES), BF16)
    to_far = ((LAYERS, across + 1, LINES, LANES), BF16)
    to_all = ((NEAR, across, LINES, LANES), BF16)

    out, grads, base = call(
        first_rows,
        [to_x, (grads.shape, grads.dtype), block],
        pltpu.with_memory_space_constraint(grads, pltpu.HBM),
        pltpu.with_memory_space_constraint(base, pltpu.HBM),
        inputs=HBM,
        scratch=[pltpu.SemaphoreType.DMA((2,))],
    )
    (mine,) = call(functools.partial(x_total, 1), [to_half], exchanged(out, "feat", X_GROUPS))
    other = lax.ppermute(mine, "feat", SWAP)
    rows0, norm0, out = call(
        first_image, [block_rows, row, to_near], grads, scaled, mine, other
    )
    (out,) = call(near_total, [to_far], exchanged(out, "samp", NEAR_GROUPS))
    resid_own, alpha0, out = call(
        first_step, [part, row, to_all], base, norm0, exchanged(out, "samp", FAR_GROUPS)
    )
    resid, out = call(
        next_rows, [block, to_x], grads, base, exchanged(out, "samp", NEAR_GROUPS)
    )
    (mine,) = call(functools.partial(x_total, 2), [to_half], exchanged(out, "feat", X_GROUPS))
    other = lax.ppermute(mine, "feat", SWAP)
    rows1, norm1, square, beta, out = call(
        next_image,
        [block_rows, row, row, row, to_near],
        grads,
        scaled,
        mine,
        other,
        rows0,
        norm0,
    )
    (out,) = call(near_total, [to_far], exchanged(out, "samp", NEAR_GROUPS))
    alpha1, out = call(
        last_step,
        [row, to_all],
        base,
        resid_own,
        norm1,
        square,
        beta,
        exchanged(out, "samp", FAR_GROUPS),
    )
    scores, answer, last = call(
        functools.partial(outputs, 1.0 / math.sqrt(m * n_feat)),
        [((share, dirs), F32), block, block],
        base,
        resid,
        beta,
        alpha0,
        alpha1,
        rows0,
        rows1,
        exchanged(out, "samp", NEAR_GROUPS),
        results=HBM,
        scratch=[
            pltpu.VMEM((share, dirs), F32),
            pltpu.VMEM((dirs, m), F32),
            pltpu.VMEM((dirs, m), F32),
            pltpu.SemaphoreType.DMA((3,)),
        ],
    )
    return scores, answer.T, last.T


def solution(mesh):
    return jax.shard_map(
        per_device,
        mesh=mesh,
        in_specs=(P("samp", "feat"), P("samp"), P("feat", None)),
        out_specs=(P(("samp", "feat"), None), P("feat", None), P("feat", None)),
        check_vma=False,
    )
```

```python
import functools
import math

import jax
import jax.numpy as jnp
from jax import lax
from jax.experimental import pallas as pl
from jax.experimental.pallas import tpu as pltpu
from jax.sharding import PartitionSpec as P

DAMPING = 0.1
PLANES, LAYERS, CORES = 4, 8, 2
HALVES, COLUMNS = 2, 4
NEAR = PLANES * CORES
LINES, LANES = 8, 128

X_GROUPS = [[h * COLUMNS + i for i in range(COLUMNS)] for h in range(HALVES)]
SWAP = [(i, (i + COLUMNS) % (HALVES * COLUMNS)) for i in range(HALVES * COLUMNS)]
FAR_ORDER = (3, 7, 0, 6, 1, 5, 2, 4)
NEAR_ORDER = ((0, 1), (1, 0), (2, 1), (3, 0), (0, 0), (1, 1), (2, 0), (3, 1))
NEAR_GROUPS = [[(y * LAYERS + z) * CORES + c for y, c in NEAR_ORDER] for z in range(LAYERS)]
FAR_GROUPS = [
    [(y * LAYERS + z) * CORES + c for z in FAR_ORDER] for y in range(PLANES) for c in range(CORES)
]
F32, BF16 = jnp.float32, jnp.bfloat16


def dot(a, b, dims):
    return lax.dot_general(a.astype(BF16), b, (dims, ((), ())), preferred_element_type=F32)


def col(x):
    return jnp.sum(x, axis=1, keepdims=True)


def iota(shape, axis):
    return lax.broadcasted_iota(jnp.int32, shape, axis)


def as_row(column):
    shape = (column.shape[0], LANES)
    eye = iota(shape, 0) == iota(shape, 1)
    return jnp.sum(jnp.where(eye, jnp.broadcast_to(column, shape), 0.0), axis=0, keepdims=True)


def as_column(row, n, first=0):
    shape = (n, LANES)
    eye = iota(shape, 0) + first == iota(shape, 1)
    return col(jnp.where(eye, jnp.broadcast_to(row, shape), 0.0))


def tail_of(*rows):
    shape = (LINES, LANES)
    tail = jnp.zeros(shape, F32)
    for i, x in enumerate(rows):
        x = jnp.broadcast_to(x, shape)
        for term in range(3):
            part = x.astype(BF16).astype(F32)
            tail = jnp.where(iota(shape, 0) == 3 * i + term, part, tail)
            x = x - part
    return tail


def row_in(tail, i):
    line = iota(tail.shape, 0)
    chosen = (line >= 3 * i) & (line < 3 * i + 3)
    return jnp.sum(jnp.where(chosen, tail, 0.0), axis=0, keepdims=True)


def tiles_of(body):
    return [
        body[i : i + LINES, j : j + LANES]
        for i in range(0, body.shape[0], LINES)
        for j in range(0, body.shape[1], LANES)
    ]


def body_of(tiles, width):
    across = width // LANES
    lines = [
        jnp.concatenate(tiles[i : i + across], axis=1) for i in range(0, len(tiles), across)
    ]
    return jnp.concatenate(lines, axis=0) if len(lines) > 1 else lines[0]


def put(ref, tiles):
    for i, tile in enumerate(tiles):
        ref[i] = tile.astype(BF16)


def put_copies(ref, tiles):
    for i in range(ref.shape[0]):
        put(ref.at[i], tiles)


def tiles_in(ref):
    return [ref[i].astype(F32) for i in range(ref.shape[0])]


def summed(ref):
    totals = tiles_in(ref.at[0])
    for i in range(1, ref.shape[0]):
        totals = [a + b for a, b in zip(totals, tiles_in(ref.at[i]))]
    return totals


def own_first():
    me = lax.axis_index("samp")
    y, c = me // (LAYERS * CORES), lax.rem(me, CORES)
    first = jnp.int32(0)
    for place, (plane, core) in enumerate(NEAR_ORDER):
        first = jnp.where((y == plane) & (c == core), place * LINES, first)
    return first


def own_lines(ref):
    return ref[pl.ds(pl.multiple_of(own_first(), LINES), LINES), :]


def put_pieces(out, image, curve):
    tiles, tail = tiles_of(image), tail_of(as_row(curve))
    across = len(tiles) // out.shape[0]
    for i in range(out.shape[0]):
        put(out.at[i], tiles[i * across : (i + 1) * across] + [tail])


def first_rows(total, grads, base, weights, out, held, line, scaled, sems):
    loads = [
        pltpu.make_async_copy(base, line, sems.at[0]),
        pltpu.make_async_copy(grads, held, sems.at[1]),
        pltpu.make_async_copy(weights, scaled, sems.at[2]),
    ]
    for load in loads:
        load.start()
    loads[0].wait()
    b = line[...]
    tail = tail_of(as_row(col(b * b)))
    packed = b.astype(BF16)
    loads[2].wait()
    scaled[...] = scaled[...] / total
    loads[1].wait()
    put(out, tiles_of(dot(packed, held[...], ((1,), (1,)))) + [tail])


def half_total(count, mine, other, out):
    tiles = [a + b for a, b in zip(tiles_in(mine), tiles_in(other))]
    tail = tail_of(*[row_in(tiles[-1], i) for i in range(count)])
    put_copies(out, tiles[:-1] + [tail])


def first_image(grads, weights, arrived, rows, norm, out):
    tiles = summed(arrived)
    r = body_of(tiles[:-1], rows.shape[1])
    rows[...] = r
    norm[...] = row_in(tiles[-1], 0)
    weighted = r * weights[...]
    put_pieces(out, dot(weighted, grads[...], ((1,), (0,))), col(weighted * r))


def near_total(arrived, out):
    tiles = summed(arrived)
    put_copies(out, tiles[:-1] + [tail_of(row_in(tiles[-1], 0))])


def first_step(base, norm, arrived, resid, alpha, out):
    tiles = summed(arrived)
    n = norm[...]
    a = n / (row_in(tiles[-1], 0) + DAMPING * n)
    alpha[...] = a
    b = own_lines(base)
    image = body_of(tiles[:-1], base.shape[1])
    r = b - as_column(a, LINES, own_first()) * (image + DAMPING * b)
    resid[...] = r
    put_copies(out, tiles_of(r))


def laid_out(arrived, width):
    return body_of([t for i in range(arrived.shape[0]) for t in tiles_in(arrived.at[i])], width)


def next_rows(grads, base, arrived, resid, out):
    b = base[...]
    r = laid_out(arrived, b.shape[1])
    resid[...] = r
    tail = tail_of(as_row(col(r * r)), as_row(col(r * b)))
    put(out, tiles_of(dot(r, grads[...], ((1,), (1,)))) + [tail])


def next_image(grads, weights, arrived, rows0, norm0, rows, norm, square, beta, out):
    tiles = summed(arrived)
    n0, n1, cross = norm0[...], row_in(tiles[-1], 0), row_in(tiles[-1], 1)
    bt = n1 / n0
    norm[...] = n1
    beta[...] = bt
    square[...] = n1 + 2.0 * bt * cross + bt * bt * n0
    old = rows0[...]
    r = body_of(tiles[:-1], old.shape[1]) + as_column(bt, old.shape[0]) * old
    rows[...] = r
    weighted = r * weights[...]
    put_pieces(out, dot(weighted, grads[...], ((1,), (0,))), col(weighted * r))


def last_step(base, resid, norm, square, beta, arrived, alpha, out):
    tiles = summed(arrived)
    a = norm[...] / (row_in(tiles[-1], 0) + DAMPING * square[...])
    alpha[...] = a
    first = own_first()
    line = resid[...] + as_column(beta[...], LINES, first) * own_lines(base)
    image = body_of(tiles[:-1], base.shape[1])
    r = resid[...] - as_column(a, LINES, first) * (image + DAMPING * line)
    put_copies(out, tiles_of(r))


def outputs(
    scale, base, resid, beta, alpha0, alpha1, rows0, rows1, arrived, scores, answer, last, *scratch
):
    score_held, answer_held, last_held, sems = scratch
    last_held[...] = laid_out(arrived, base.shape[1])
    stores = [
        pltpu.make_async_copy(held, out, sems.at[i])
        for i, (held, out) in enumerate(
            ((last_held, last), (answer_held, answer), (score_held, scores))
        )
    ]
    stores[0].start()
    b = base[...]
    dirs = b.shape[0]
    a0, a1 = as_column(alpha0[...], dirs), as_column(alpha1[...], dirs)
    answer_held[...] = a0 * b + a1 * (resid[...] + as_column(beta[...], dirs) * b)
    stores[1].start()
    every = (a0 * rows0[...] + a1 * rows1[...]) * scale
    share = scores.shape[0]
    feat = lax.axis_index("feat")
    mine = every[:, :share]
    for i in range(1, every.shape[1] // share):
        mine = jnp.where(feat == i, every[:, i * share : (i + 1) * share], mine)
    score_held[...] = mine.T
    stores[2].start()
    for store in stores:
        store.wait()


VMEM = pl.BlockSpec(memory_space=pltpu.VMEM)
HBM = pl.BlockSpec(memory_space=pltpu.HBM)


def call(kernel, outs, *args, inputs=VMEM, results=VMEM, scratch=()):
    return pl.pallas_call(
        kernel,
        out_shape=[jax.ShapeDtypeStruct(s, t) for s, t in outs],
        in_specs=[inputs] * len(args),
        out_specs=[results] * len(outs),
        scratch_shapes=list(scratch),
        compiler_params=pltpu.CompilerParams(vmem_limit_bytes=8 * 2**20),
    )(*args)


def exchanged(pieces, axis, groups):
    return lax.all_to_all(pieces, axis, 0, 0, tiled=True, axis_index_groups=groups)


def per_device(grads, weights, targets):
    n_samp, n_feat = lax.axis_size("samp"), lax.axis_size("feat")
    samples = grads.shape[0]
    share = samples // n_feat
    base = targets.T
    dirs, m = base.shape
    across = m // LANES
    row_tiles = dirs // LINES * (samples // LANES) + 1
    block, row, part = ((dirs, m), F32), ((1, LANES), F32), ((LINES, m), F32)
    block_rows = ((dirs, samples), F32)
    to_x = ((COLUMNS, row_tiles, LINES, LANES), BF16)
    to_half = ((row_tiles, LINES, LANES), BF16)
    to_near = ((NEAR, across + 1, LINES, LANES), BF16)
    to_far = ((LAYERS, across + 1, LINES, LANES), BF16)
    to_all = ((NEAR, across, LINES, LANES), BF16)

    out, grads, base, scaled = call(
        functools.partial(first_rows, samples * n_samp),
        [to_half, (grads.shape, grads.dtype), block, ((1, samples), F32)],
        pltpu.with_memory_space_constraint(grads, pltpu.HBM),
        pltpu.with_memory_space_constraint(base, pltpu.HBM),
        pltpu.with_memory_space_constraint(weights[None, :], pltpu.HBM),
        inputs=HBM,
        scratch=[pltpu.SemaphoreType.DMA((3,))],
    )
    other = lax.ppermute(out, "feat", SWAP)
    (out,) = call(functools.partial(half_total, 1), [to_x], out, other)
    rows0, norm0, out = call(
        first_image, [block_rows, row, to_near], grads, scaled, exchanged(out, "feat", X_GROUPS)
    )
    (out,) = call(near_total, [to_far], exchanged(out, "samp", NEAR_GROUPS))
    resid_own, alpha0, out = call(
        first_step, [part, row, to_all], base, norm0, exchanged(out, "samp", FAR_GROUPS)
    )
    resid, out = call(
        next_rows, [block, to_half], grads, base, exchanged(out, "samp", NEAR_GROUPS)
    )
    other = lax.ppermute(out, "feat", SWAP)
    (out,) = call(functools.partial(half_total, 2), [to_x], out, other)
    rows1, norm1, square, beta, out = call(
        next_image,
        [block_rows, row, row, row, to_near],
        grads,
        scaled,
        exchanged(out, "feat", X_GROUPS),
        rows0,
        norm0,
    )
    (out,) = call(near_total, [to_far], exchanged(out, "samp", NEAR_GROUPS))
    alpha1, out = call(
        last_step,
        [row, to_all],
        base,
        resid_own,
        norm1,
        square,
        beta,
        exchanged(out, "samp", FAR_GROUPS),
    )
    scores, answer, last = call(
        functools.partial(outputs, 1.0 / math.sqrt(m * n_feat)),
        [((share, dirs), F32), block, block],
        base,
        resid,
        beta,
        alpha0,
        alpha1,
        rows0,
        rows1,
        exchanged(out, "samp", NEAR_GROUPS),
        results=HBM,
        scratch=[
            pltpu.VMEM((share, dirs), F32),
            pltpu.VMEM((dirs, m), F32),
            pltpu.VMEM((dirs, m), F32),
            pltpu.SemaphoreType.DMA((3,)),
        ],
    )
    return scores, answer.T, last.T


def solution(mesh):
    return jax.shard_map(
        per_device,
        mesh=mesh,
        in_specs=(P("samp", "feat"), P("samp"), P("feat", None)),
        out_specs=(P(("samp", "feat"), None), P("feat", None), P("feat", None)),
        check_vma=False,
    )
```

```python
import functools
import math

import jax
import jax.numpy as jnp
from jax import lax
from jax.experimental import pallas as pl
from jax.experimental.pallas import tpu as pltpu
from jax.sharding import PartitionSpec as P

DAMPING = 0.1
PLANES, LAYERS, CORES = 4, 8, 2
HALVES, COLUMNS = 2, 4
NEAR = PLANES * CORES
LINES, LANES = 8, 128

X_GROUPS = [[h * COLUMNS + i for i in range(COLUMNS)] for h in range(HALVES)]
FEAT_ORDER = (0, 6, 1, 4, 2, 5, 3, 7)
FAR_ORDER = (3, 7, 0, 6, 1, 5, 2, 4)
NEAR_ORDER = ((0, 1), (1, 0), (2, 1), (3, 0), (0, 0), (1, 1), (2, 0), (3, 1))
NEAR_GROUPS = [[(y * LAYERS + z) * CORES + c for y, c in NEAR_ORDER] for z in range(LAYERS)]
FAR_GROUPS = [
    [(y * LAYERS + z) * CORES + c for z in FAR_ORDER] for y in range(PLANES) for c in range(CORES)
]
F32, BF16 = jnp.float32, jnp.bfloat16


def dot(a, b, dims):
    return lax.dot_general(a.astype(BF16), b, (dims, ((), ())), preferred_element_type=F32)


def col(x):
    return jnp.sum(x, axis=1, keepdims=True)


def iota(shape, axis):
    return lax.broadcasted_iota(jnp.int32, shape, axis)


def as_row(column):
    shape = (column.shape[0], LANES)
    eye = iota(shape, 0) == iota(shape, 1)
    return jnp.sum(jnp.where(eye, jnp.broadcast_to(column, shape), 0.0), axis=0, keepdims=True)


def as_column(row, n, first=0):
    shape = (n, LANES)
    eye = iota(shape, 0) + first == iota(shape, 1)
    return col(jnp.where(eye, jnp.broadcast_to(row, shape), 0.0))


def tail_of(*rows):
    shape = (LINES, LANES)
    tail = jnp.zeros(shape, F32)
    for i, x in enumerate(rows):
        x = jnp.broadcast_to(x, shape)
        for term in range(3):
            part = x.astype(BF16).astype(F32)
            tail = jnp.where(iota(shape, 0) == 3 * i + term, part, tail)
            x = x - part
    return tail


def row_in(tail, i):
    line = iota(tail.shape, 0)
    chosen = (line >= 3 * i) & (line < 3 * i + 3)
    return jnp.sum(jnp.where(chosen, tail, 0.0), axis=0, keepdims=True)


def tiles_of(body):
    return [
        body[i : i + LINES, j : j + LANES]
        for i in range(0, body.shape[0], LINES)
        for j in range(0, body.shape[1], LANES)
    ]


def body_of(tiles, width):
    across = width // LANES
    lines = [
        jnp.concatenate(tiles[i : i + across], axis=1) for i in range(0, len(tiles), across)
    ]
    return jnp.concatenate(lines, axis=0) if len(lines) > 1 else lines[0]


def put(ref, tiles):
    for i, tile in enumerate(tiles):
        ref[i] = tile.astype(BF16)


def put_copies(ref, tiles):
    for i in range(ref.shape[0]):
        put(ref.at[i], tiles)


def tiles_in(ref):
    return [ref[i].astype(F32) for i in range(ref.shape[0])]


def summed(ref):
    totals = tiles_in(ref.at[0])
    for i in range(1, ref.shape[0]):
        totals = [a + b for a, b in zip(totals, tiles_in(ref.at[i]))]
    return totals


def own_first():
    me = lax.axis_index("samp")
    y, c = me // (LAYERS * CORES), lax.rem(me, CORES)
    first = jnp.int32(0)
    for place, (plane, core) in enumerate(NEAR_ORDER):
        first = jnp.where((y == plane) & (c == core), place * LINES, first)
    return first


def own_lines(ref):
    return ref[pl.ds(pl.multiple_of(own_first(), LINES), LINES), :]


def put_pieces(out, image, curve):
    tiles, tail = tiles_of(image), tail_of(as_row(curve))
    across = len(tiles) // out.shape[0]
    for i in range(out.shape[0]):
        put(out.at[i], tiles[i * across : (i + 1) * across] + [tail])


def put_quarters(out, tiles, tail):
    each = len(tiles) // out.shape[0]
    for i in range(out.shape[0]):
        put(out.at[i], tiles[i * each : (i + 1) * each] + [tail])


def first_rows(total, grads, base, weights, out, held, line, scaled, sems):
    loads = [
        pltpu.make_async_copy(base, line, sems.at[0]),
        pltpu.make_async_copy(grads, held, sems.at[1]),
        pltpu.make_async_copy(weights, scaled, sems.at[2]),
    ]
    for load in loads:
        load.start()
    loads[0].wait()
    b = line[...]
    tail = tail_of(as_row(col(b * b)))
    packed = b.astype(BF16)
    loads[2].wait()
    scaled[...] = scaled[...] / total
    loads[1].wait()
    put_quarters(out, tiles_of(dot(packed, held[...], ((1,), (1,)))), tail)


def x_total(count, arrived, out):
    tiles = summed(arrived)
    tail = tail_of(*[row_in(tiles[-1], i) for i in range(count)])
    put_copies(out, tiles[:-1] + [tail])


def feat_total(arrived):
    tiles, tail = [], None
    for x in range(COLUMNS):
        low, high = (arrived.at[FEAT_ORDER.index(half * COLUMNS + x)] for half in range(HALVES))
        both = [a + b for a, b in zip(tiles_in(low), tiles_in(high))]
        tiles += both[:-1]
        tail = both[-1] if x == 0 else tail
    return tiles + [tail]


def first_image(grads, weights, arrived, rows, norm, out):
    tiles = feat_total(arrived)
    r = body_of(tiles[:-1], rows.shape[1])
    rows[...] = r
    norm[...] = row_in(tiles[-1], 0)
    weighted = r * weights[...]
    put_pieces(out, dot(weighted, grads[...], ((1,), (0,))), col(weighted * r))


def near_total(arrived, out):
    tiles = summed(arrived)
    put_copies(out, tiles[:-1] + [tail_of(row_in(tiles[-1], 0))])


def first_step(base, norm, arrived, resid, alpha, out):
    tiles = summed(arrived)
    n = norm[...]
    a = n / (row_in(tiles[-1], 0) + DAMPING * n)
    alpha[...] = a
    b = own_lines(base)
    image = body_of(tiles[:-1], base.shape[1])
    r = b - as_column(a, LINES, own_first()) * (image + DAMPING * b)
    resid[...] = r
    put_copies(out, tiles_of(r))


def laid_out(arrived, width):
    return body_of([t for i in range(arrived.shape[0]) for t in tiles_in(arrived.at[i])], width)


def next_rows(grads, base, arrived, resid, out):
    b = base[...]
    r = laid_out(arrived, b.shape[1])
    resid[...] = r
    tail = tail_of(as_row(col(r * r)), as_row(col(r * b)))
    put_quarters(out, tiles_of(dot(r, grads[...], ((1,), (1,)))), tail)


def next_image(grads, weights, arrived, rows0, norm0, rows, norm, square, beta, out):
    tiles = feat_total(arrived)
    n0, n1, cross = norm0[...], row_in(tiles[-1], 0), row_in(tiles[-1], 1)
    bt = n1 / n0
    norm[...] = n1
    beta[...] = bt
    square[...] = n1 + 2.0 * bt * cross + bt * bt * n0
    old = rows0[...]
    r = body_of(tiles[:-1], old.shape[1]) + as_column(bt, old.shape[0]) * old
    rows[...] = r
    weighted = r * weights[...]
    put_pieces(out, dot(weighted, grads[...], ((1,), (0,))), col(weighted * r))


def last_step(base, resid, norm, square, beta, arrived, alpha, out):
    tiles = summed(arrived)
    a = norm[...] / (row_in(tiles[-1], 0) + DAMPING * square[...])
    alpha[...] = a
    first = own_first()
    line = resid[...] + as_column(beta[...], LINES, first) * own_lines(base)
    image = body_of(tiles[:-1], base.shape[1])
    r = resid[...] - as_column(a, LINES, first) * (image + DAMPING * line)
    put_copies(out, tiles_of(r))


def outputs(
    scale, base, resid, beta, alpha0, alpha1, rows0, rows1, arrived, scores, answer, last, *scratch
):
    score_held, answer_held, last_held, sems = scratch
    last_held[...] = laid_out(arrived, base.shape[1])
    stores = [
        pltpu.make_async_copy(held, out, sems.at[i])
        for i, (held, out) in enumerate(
            ((last_held, last), (answer_held, answer), (score_held, scores))
        )
    ]
    stores[0].start()
    b = base[...]
    dirs = b.shape[0]
    a0, a1 = as_column(alpha0[...], dirs), as_column(alpha1[...], dirs)
    answer_held[...] = a0 * b + a1 * (resid[...] + as_column(beta[...], dirs) * b)
    stores[1].start()
    every = (a0 * rows0[...] + a1 * rows1[...]) * scale
    share = scores.shape[0]
    feat = lax.axis_index("feat")
    mine = every[:, :share]
    for i in range(1, every.shape[1] // share):
        mine = jnp.where(feat == i, every[:, i * share : (i + 1) * share], mine)
    score_held[...] = mine.T
    stores[2].start()
    for store in stores:
        store.wait()


VMEM = pl.BlockSpec(memory_space=pltpu.VMEM)
HBM = pl.BlockSpec(memory_space=pltpu.HBM)


def call(kernel, outs, *args, inputs=VMEM, results=VMEM, scratch=()):
    return pl.pallas_call(
        kernel,
        out_shape=[jax.ShapeDtypeStruct(s, t) for s, t in outs],
        in_specs=[inputs] * len(args),
        out_specs=[results] * len(outs),
        scratch_shapes=list(scratch),
        compiler_params=pltpu.CompilerParams(vmem_limit_bytes=8 * 2**20),
    )(*args)


def exchanged(pieces, axis, groups):
    return lax.all_to_all(pieces, axis, 0, 0, tiled=True, axis_index_groups=groups)


def per_device(grads, weights, targets):
    n_samp, n_feat = lax.axis_size("samp"), lax.axis_size("feat")
    samples = grads.shape[0]
    share = samples // n_feat
    base = targets.T
    dirs, m = base.shape
    across = m // LANES
    quarter = dirs // COLUMNS // LINES * (samples // LANES) + 1
    block, row, part = ((dirs, m), F32), ((1, LANES), F32), ((LINES, m), F32)
    block_rows = ((dirs, samples), F32)
    to_x = ((COLUMNS, quarter, LINES, LANES), BF16)
    to_feat = ((HALVES * COLUMNS, quarter, LINES, LANES), BF16)
    to_near = ((NEAR, across + 1, LINES, LANES), BF16)
    to_far = ((LAYERS, across + 1, LINES, LANES), BF16)
    to_all = ((NEAR, across, LINES, LANES), BF16)

    out, grads, base, scaled = call(
        functools.partial(first_rows, samples * n_samp),
        [to_x, (grads.shape, grads.dtype), block, ((1, samples), F32)],
        pltpu.with_memory_space_constraint(grads, pltpu.HBM),
        pltpu.with_memory_space_constraint(base, pltpu.HBM),
        pltpu.with_memory_space_constraint(weights[None, :], pltpu.HBM),
        inputs=HBM,
        scratch=[pltpu.SemaphoreType.DMA((3,))],
    )
    (out,) = call(functools.partial(x_total, 1), [to_feat], exchanged(out, "feat", X_GROUPS))
    rows0, norm0, out = call(
        first_image, [block_rows, row, to_near], grads, scaled, exchanged(out, "feat", [FEAT_ORDER])
    )
    (out,) = call(near_total, [to_far], exchanged(out, "samp", NEAR_GROUPS))
    resid_own, alpha0, out = call(
        first_step, [part, row, to_all], base, norm0, exchanged(out, "samp", FAR_GROUPS)
    )
    resid, out = call(
        next_rows, [block, to_x], grads, base, exchanged(out, "samp", NEAR_GROUPS)
    )
    (out,) = call(functools.partial(x_total, 2), [to_feat], exchanged(out, "feat", X_GROUPS))
    rows1, norm1, square, beta, out = call(
        next_image,
        [block_rows, row, row, row, to_near],
        grads,
        scaled,
        exchanged(out, "feat", [FEAT_ORDER]),
        rows0,
        norm0,
    )
    (out,) = call(near_total, [to_far], exchanged(out, "samp", NEAR_GROUPS))
    alpha1, out = call(
        last_step,
        [row, to_all],
        base,
        resid_own,
        norm1,
        square,
        beta,
        exchanged(out, "samp", FAR_GROUPS),
    )
    scores, answer, last = call(
        functools.partial(outputs, 1.0 / math.sqrt(m * n_feat)),
        [((share, dirs), F32), block, block],
        base,
        resid,
        beta,
        alpha0,
        alpha1,
        rows0,
        rows1,
        exchanged(out, "samp", NEAR_GROUPS),
        results=HBM,
        scratch=[
            pltpu.VMEM((share, dirs), F32),
            pltpu.VMEM((dirs, m), F32),
            pltpu.VMEM((dirs, m), F32),
            pltpu.SemaphoreType.DMA((3,)),
        ],
    )
    return scores, answer.T, last.T


def solution(mesh):
    return jax.shard_map(
        per_device,
        mesh=mesh,
        in_specs=(P("samp", "feat"), P("samp"), P("feat", None)),
        out_specs=(P(("samp", "feat"), None), P("feat", None), P("feat", None)),
        check_vma=False,
    )
```

```python
import functools
import math

import jax
import jax.numpy as jnp
from jax import lax
from jax.experimental import pallas as pl
from jax.experimental.pallas import tpu as pltpu
from jax.sharding import PartitionSpec as P

DAMPING = 0.1
PLANES, LAYERS, CORES = 4, 8, 2
HALVES, COLUMNS = 2, 4
NEAR = PLANES * CORES
LINES, LANES = 8, 128

X_GROUPS = [[h * COLUMNS + i for i in range(COLUMNS)] for h in range(HALVES)]
SWAP = [(i, (i + COLUMNS) % (HALVES * COLUMNS)) for i in range(HALVES * COLUMNS)]
FAR_ORDER = (3, 7, 0, 6, 1, 5, 2, 4)
NEAR_ORDER = ((1, 1), (2, 0), (0, 1), (3, 0), (1, 0), (2, 1), (0, 0), (3, 1))
NEAR_GROUPS = [[(y * LAYERS + z) * CORES + c for y, c in NEAR_ORDER] for z in range(LAYERS)]
FAR_GROUPS = [
    [(y * LAYERS + z) * CORES + c for z in FAR_ORDER] for y in range(PLANES) for c in range(CORES)
]
F32, BF16 = jnp.float32, jnp.bfloat16


def dot(a, b, dims):
    return lax.dot_general(a.astype(BF16), b, (dims, ((), ())), preferred_element_type=F32)


def col(x):
    return jnp.sum(x, axis=1, keepdims=True)


def iota(shape, axis):
    return lax.broadcasted_iota(jnp.int32, shape, axis)


def as_row(column):
    shape = (column.shape[0], LANES)
    eye = iota(shape, 0) == iota(shape, 1)
    return jnp.sum(jnp.where(eye, jnp.broadcast_to(column, shape), 0.0), axis=0, keepdims=True)


def as_column(row, n, first=0):
    shape = (n, LANES)
    eye = iota(shape, 0) + first == iota(shape, 1)
    return col(jnp.where(eye, jnp.broadcast_to(row, shape), 0.0))


def tail_of(*rows):
    shape = (LINES, LANES)
    tail = jnp.zeros(shape, F32)
    for i, x in enumerate(rows):
        x = jnp.broadcast_to(x, shape)
        for term in range(3):
            part = x.astype(BF16).astype(F32)
            tail = jnp.where(iota(shape, 0) == 3 * i + term, part, tail)
            x = x - part
    return tail


def row_in(tail, i):
    line = iota(tail.shape, 0)
    chosen = (line >= 3 * i) & (line < 3 * i + 3)
    return jnp.sum(jnp.where(chosen, tail, 0.0), axis=0, keepdims=True)


def tiles_of(body):
    return [
        body[i : i + LINES, j : j + LANES]
        for i in range(0, body.shape[0], LINES)
        for j in range(0, body.shape[1], LANES)
    ]


def body_of(tiles, width):
    across = width // LANES
    lines = [
        jnp.concatenate(tiles[i : i + across], axis=1) for i in range(0, len(tiles), across)
    ]
    return jnp.concatenate(lines, axis=0) if len(lines) > 1 else lines[0]


def put(ref, tiles):
    for i, tile in enumerate(tiles):
        ref[i] = tile.astype(BF16)


def put_copies(ref, tiles):
    for i in range(ref.shape[0]):
        put(ref.at[i], tiles)


def tiles_in(ref):
    return [ref[i].astype(F32) for i in range(ref.shape[0])]


def summed(ref):
    totals = tiles_in(ref.at[0])
    for i in range(1, ref.shape[0]):
        totals = [a + b for a, b in zip(totals, tiles_in(ref.at[i]))]
    return totals


def own_first():
    me = lax.axis_index("samp")
    y, c = me // (LAYERS * CORES), lax.rem(me, CORES)
    first = jnp.int32(0)
    for place, (plane, core) in enumerate(NEAR_ORDER):
        first = jnp.where((y == plane) & (c == core), place * LINES, first)
    return first


def own_lines(ref):
    return ref[pl.ds(pl.multiple_of(own_first(), LINES), LINES), :]


def put_pieces(out, image, curve):
    tiles, tail = tiles_of(image), tail_of(as_row(curve))
    across = len(tiles) // out.shape[0]
    for i in range(out.shape[0]):
        put(out.at[i], tiles[i * across : (i + 1) * across] + [tail])


def first_rows(grads, base, out, held, line, sems):
    loads = [
        pltpu.make_async_copy(base, line, sems.at[0]),
        pltpu.make_async_copy(grads, held, sems.at[1]),
    ]
    for load in loads:
        load.start()
    loads[0].wait()
    b = line[...]
    tail = tail_of(as_row(col(b * b)))
    packed = b.astype(BF16)
    loads[1].wait()
    put_copies(out, tiles_of(dot(packed, held[...], ((1,), (1,)))) + [tail])


def x_total(count, arrived, out):
    tiles = summed(arrived)
    tail = tail_of(*[row_in(tiles[-1], i) for i in range(count)])
    put(out, tiles[:-1] + [tail])


def first_image(grads, weights, mine, other, rows, norm, out):
    tiles = [a + b for a, b in zip(tiles_in(mine), tiles_in(other))]
    r = body_of(tiles[:-1], rows.shape[1])
    rows[...] = r
    norm[...] = row_in(tiles[-1], 0)
    weighted = r * weights[...]
    put_pieces(out, dot(weighted, grads[...], ((1,), (0,))), col(weighted * r))


def near_total(arrived, out):
    tiles = summed(arrived)
    put_copies(out, tiles[:-1] + [tail_of(row_in(tiles[-1], 0))])


def first_step(base, norm, arrived, resid, alpha, out):
    tiles = summed(arrived)
    n = norm[...]
    a = n / (row_in(tiles[-1], 0) + DAMPING * n)
    alpha[...] = a
    b = own_lines(base)
    image = body_of(tiles[:-1], base.shape[1])
    r = b - as_column(a, LINES, own_first()) * (image + DAMPING * b)
    resid[...] = r
    put_copies(out, tiles_of(r))


def laid_out(arrived, width):
    return body_of([t for i in range(arrived.shape[0]) for t in tiles_in(arrived.at[i])], width)


def next_rows(grads, base, arrived, resid, out):
    b = base[...]
    r = laid_out(arrived, b.shape[1])
    resid[...] = r
    tail = tail_of(as_row(col(r * r)), as_row(col(r * b)))
    put_copies(out, tiles_of(dot(r, grads[...], ((1,), (1,)))) + [tail])


def next_image(grads, weights, mine, other, rows0, norm0, rows, norm, square, beta, out):
    tiles = [a + b for a, b in zip(tiles_in(mine), tiles_in(other))]
    n0, n1, cross = norm0[...], row_in(tiles[-1], 0), row_in(tiles[-1], 1)
    bt = n1 / n0
    norm[...] = n1
    beta[...] = bt
    square[...] = n1 + 2.0 * bt * cross + bt * bt * n0
    old = rows0[...]
    r = body_of(tiles[:-1], old.shape[1]) + as_column(bt, old.shape[0]) * old
    rows[...] = r
    weighted = r * weights[...]
    put_pieces(out, dot(weighted, grads[...], ((1,), (0,))), col(weighted * r))


def last_step(base, resid, norm, square, beta, arrived, alpha, out):
    tiles = summed(arrived)
    a = norm[...] / (row_in(tiles[-1], 0) + DAMPING * square[...])
    alpha[...] = a
    first = own_first()
    line = resid[...] + as_column(beta[...], LINES, first) * own_lines(base)
    image = body_of(tiles[:-1], base.shape[1])
    r = resid[...] - as_column(a, LINES, first) * (image + DAMPING * line)
    put_copies(out, tiles_of(r))


def outputs(
    scale, base, resid, beta, alpha0, alpha1, rows0, rows1, arrived, scores, answer, last, *scratch
):
    score_held, answer_held, last_held, sems = scratch
    last_held[...] = laid_out(arrived, base.shape[1])
    stores = [
        pltpu.make_async_copy(held, out, sems.at[i])
        for i, (held, out) in enumerate(
            ((last_held, last), (answer_held, answer), (score_held, scores))
        )
    ]
    stores[0].start()
    b = base[...]
    dirs = b.shape[0]
    a0, a1 = as_column(alpha0[...], dirs), as_column(alpha1[...], dirs)
    answer_held[...] = a0 * b + a1 * (resid[...] + as_column(beta[...], dirs) * b)
    stores[1].start()
    every = (a0 * rows0[...] + a1 * rows1[...]) * scale
    share = scores.shape[0]
    feat = lax.axis_index("feat")
    mine = every[:, :share]
    for i in range(1, every.shape[1] // share):
        mine = jnp.where(feat == i, every[:, i * share : (i + 1) * share], mine)
    score_held[...] = mine.T
    stores[2].start()
    for store in stores:
        store.wait()


VMEM = pl.BlockSpec(memory_space=pltpu.VMEM)
HBM = pl.BlockSpec(memory_space=pltpu.HBM)


def call(kernel, outs, *args, inputs=VMEM, results=VMEM, scratch=()):
    return pl.pallas_call(
        kernel,
        out_shape=[jax.ShapeDtypeStruct(s, t) for s, t in outs],
        in_specs=[inputs] * len(args),
        out_specs=[results] * len(outs),
        scratch_shapes=list(scratch),
        compiler_params=pltpu.CompilerParams(vmem_limit_bytes=8 * 2**20),
    )(*args)


def exchanged(pieces, axis, groups):
    return lax.all_to_all(pieces, axis, 0, 0, tiled=True, axis_index_groups=groups)


def per_device(grads, weights, targets):
    n_samp, n_feat = lax.axis_size("samp"), lax.axis_size("feat")
    samples = grads.shape[0]
    share = samples // n_feat
    scaled = (weights / (samples * n_samp))[None, :]
    base = targets.T
    dirs, m = base.shape
    across = m // LANES
    row_tiles = dirs // LINES * (samples // LANES) + 1
    block, row, part = ((dirs, m), F32), ((1, LANES), F32), ((LINES, m), F32)
    block_rows = ((dirs, samples), F32)
    to_x = ((COLUMNS, row_tiles, LINES, LANES), BF16)
    to_half = ((row_tiles, LINES, LANES), BF16)
    to_near = ((NEAR, across + 1, LINES, LANES), BF16)
    to_far = ((LAYERS, across + 1, LINES, LANES), BF16)
    to_all = ((NEAR, across, LINES, LANES), BF16)

    out, grads, base = call(
        first_rows,
        [to_x, (grads.shape, grads.dtype), block],
        pltpu.with_memory_space_constraint(grads, pltpu.HBM),
        pltpu.with_memory_space_constraint(base, pltpu.HBM),
        inputs=HBM,
        scratch=[pltpu.SemaphoreType.DMA((2,))],
    )
    (mine,) = call(functools.partial(x_total, 1), [to_half], exchanged(out, "feat", X_GROUPS))
    other = lax.ppermute(mine, "feat", SWAP)
    rows0, norm0, out = call(
        first_image, [block_rows, row, to_near], grads, scaled, mine, other
    )
    (out,) = call(near_total, [to_far], exchanged(out, "samp", NEAR_GROUPS))
    resid_own, alpha0, out = call(
        first_step, [part, row, to_all], base, norm0, exchanged(out, "samp", FAR_GROUPS)
    )
    resid, out = call(
        next_rows, [block, to_x], grads, base, exchanged(out, "samp", NEAR_GROUPS)
    )
    (mine,) = call(functools.partial(x_total, 2), [to_half], exchanged(out, "feat", X_GROUPS))
    other = lax.ppermute(mine, "feat", SWAP)
    rows1, norm1, square, beta, out = call(
        next_image,
        [block_rows, row, row, row, to_near],
        grads,
        scaled,
        mine,
        other,
        rows0,
        norm0,
    )
    (out,) = call(near_total, [to_far], exchanged(out, "samp", NEAR_GROUPS))
    alpha1, out = call(
        last_step,
        [row, to_all],
        base,
        resid_own,
        norm1,
        square,
        beta,
        exchanged(out, "samp", FAR_GROUPS),
    )
    scores, answer, last = call(
        functools.partial(outputs, 1.0 / math.sqrt(m * n_feat)),
        [((share, dirs), F32), block, block],
        base,
        resid,
        beta,
        alpha0,
        alpha1,
        rows0,
        rows1,
        exchanged(out, "samp", NEAR_GROUPS),
        results=HBM,
        scratch=[
            pltpu.VMEM((share, dirs), F32),
            pltpu.VMEM((dirs, m), F32),
            pltpu.VMEM((dirs, m), F32),
            pltpu.SemaphoreType.DMA((3,)),
        ],
    )
    return scores, answer.T, last.T


def solution(mesh):
    return jax.shard_map(
        per_device,
        mesh=mesh,
        in_specs=(P("samp", "feat"), P("samp"), P("feat", None)),
        out_specs=(P(("samp", "feat"), None), P("feat", None), P("feat", None)),
        check_vma=False,
    )
```

```python
import functools
import math

import jax
import jax.numpy as jnp
from jax import lax
from jax.experimental import pallas as pl
from jax.experimental.pallas import tpu as pltpu
from jax.sharding import PartitionSpec as P

DAMPING = 0.1
PLANES, LAYERS, CORES = 4, 8, 2
HALVES, COLUMNS = 2, 4
NEAR = PLANES * CORES
LINES, LANES = 8, 128

X_GROUPS = [[h * COLUMNS + i for i in range(COLUMNS)] for h in range(HALVES)]
SWAP = [(i, (i + COLUMNS) % (HALVES * COLUMNS)) for i in range(HALVES * COLUMNS)]
FAR_ORDER = (3, 7, 0, 6, 1, 5, 2, 4)
NEAR_ORDER = ((2, 0), (1, 1), (3, 0), (0, 1), (2, 1), (1, 0), (3, 1), (0, 0))
NEAR_GROUPS = [[(y * LAYERS + z) * CORES + c for y, c in NEAR_ORDER] for z in range(LAYERS)]
FAR_GROUPS = [
    [(y * LAYERS + z) * CORES + c for z in FAR_ORDER] for y in range(PLANES) for c in range(CORES)
]
F32, BF16 = jnp.float32, jnp.bfloat16


def dot(a, b, dims):
    return lax.dot_general(a.astype(BF16), b, (dims, ((), ())), preferred_element_type=F32)


def col(x):
    return jnp.sum(x, axis=1, keepdims=True)


def iota(shape, axis):
    return lax.broadcasted_iota(jnp.int32, shape, axis)


def as_row(column):
    shape = (column.shape[0], LANES)
    eye = iota(shape, 0) == iota(shape, 1)
    return jnp.sum(jnp.where(eye, jnp.broadcast_to(column, shape), 0.0), axis=0, keepdims=True)


def as_column(row, n, first=0):
    shape = (n, LANES)
    eye = iota(shape, 0) + first == iota(shape, 1)
    return col(jnp.where(eye, jnp.broadcast_to(row, shape), 0.0))


def tail_of(*rows):
    shape = (LINES, LANES)
    tail = jnp.zeros(shape, F32)
    for i, x in enumerate(rows):
        x = jnp.broadcast_to(x, shape)
        for term in range(3):
            part = x.astype(BF16).astype(F32)
            tail = jnp.where(iota(shape, 0) == 3 * i + term, part, tail)
            x = x - part
    return tail


def row_in(tail, i):
    line = iota(tail.shape, 0)
    chosen = (line >= 3 * i) & (line < 3 * i + 3)
    return jnp.sum(jnp.where(chosen, tail, 0.0), axis=0, keepdims=True)


def tiles_of(body):
    return [
        body[i : i + LINES, j : j + LANES]
        for i in range(0, body.shape[0], LINES)
        for j in range(0, body.shape[1], LANES)
    ]


def body_of(tiles, width):
    across = width // LANES
    lines = [
        jnp.concatenate(tiles[i : i + across], axis=1) for i in range(0, len(tiles), across)
    ]
    return jnp.concatenate(lines, axis=0) if len(lines) > 1 else lines[0]


def put(ref, tiles):
    for i, tile in enumerate(tiles):
        ref[i] = tile.astype(BF16)


def put_copies(ref, tiles):
    for i in range(ref.shape[0]):
        put(ref.at[i], tiles)


def tiles_in(ref):
    return [ref[i].astype(F32) for i in range(ref.shape[0])]


def summed(ref):
    totals = tiles_in(ref.at[0])
    for i in range(1, ref.shape[0]):
        totals = [a + b for a, b in zip(totals, tiles_in(ref.at[i]))]
    return totals


def own_first():
    me = lax.axis_index("samp")
    y, c = me // (LAYERS * CORES), lax.rem(me, CORES)
    first = jnp.int32(0)
    for place, (plane, core) in enumerate(NEAR_ORDER):
        first = jnp.where((y == plane) & (c == core), place * LINES, first)
    return first


def own_lines(ref):
    return ref[pl.ds(pl.multiple_of(own_first(), LINES), LINES), :]


def put_pieces(out, image, curve):
    tiles, tail = tiles_of(image), tail_of(as_row(curve))
    across = len(tiles) // out.shape[0]
    for i in range(out.shape[0]):
        put(out.at[i], tiles[i * across : (i + 1) * across] + [tail])


def first_rows(grads, base, out, held, line, sems):
    loads = [
        pltpu.make_async_copy(base, line, sems.at[0]),
        pltpu.make_async_copy(grads, held, sems.at[1]),
    ]
    for load in loads:
        load.start()
    loads[0].wait()
    b = line[...]
    tail = tail_of(as_row(col(b * b)))
    packed = b.astype(BF16)
    loads[1].wait()
    put_copies(out, tiles_of(dot(packed, held[...], ((1,), (1,)))) + [tail])


def x_total(count, arrived, out):
    tiles = summed(arrived)
    tail = tail_of(*[row_in(tiles[-1], i) for i in range(count)])
    put(out, tiles[:-1] + [tail])


def first_image(grads, weights, mine, other, rows, norm, out):
    tiles = [a + b for a, b in zip(tiles_in(mine), tiles_in(other))]
    r = body_of(tiles[:-1], rows.shape[1])
    rows[...] = r
    norm[...] = row_in(tiles[-1], 0)
    weighted = r * weights[...]
    put_pieces(out, dot(weighted, grads[...], ((1,), (0,))), col(weighted * r))


def near_total(arrived, out):
    tiles = summed(arrived)
    put_copies(out, tiles[:-1] + [tail_of(row_in(tiles[-1], 0))])


def first_step(base, norm, arrived, resid, alpha, out):
    tiles = summed(arrived)
    n = norm[...]
    a = n / (row_in(tiles[-1], 0) + DAMPING * n)
    alpha[...] = a
    b = own_lines(base)
    image = body_of(tiles[:-1], base.shape[1])
    r = b - as_column(a, LINES, own_first()) * (image + DAMPING * b)
    resid[...] = r
    put_copies(out, tiles_of(r))


def laid_out(arrived, width):
    return body_of([t for i in range(arrived.shape[0]) for t in tiles_in(arrived.at[i])], width)


def next_rows(grads, base, arrived, resid, out):
    b = base[...]
    r = laid_out(arrived, b.shape[1])
    resid[...] = r
    tail = tail_of(as_row(col(r * r)), as_row(col(r * b)))
    put_copies(out, tiles_of(dot(r, grads[...], ((1,), (1,)))) + [tail])


def next_image(grads, weights, mine, other, rows0, norm0, rows, norm, square, beta, out):
    tiles = [a + b for a, b in zip(tiles_in(mine), tiles_in(other))]
    n0, n1, cross = norm0[...], row_in(tiles[-1], 0), row_in(tiles[-1], 1)
    bt = n1 / n0
    norm[...] = n1
    beta[...] = bt
    square[...] = n1 + 2.0 * bt * cross + bt * bt * n0
    old = rows0[...]
    r = body_of(tiles[:-1], old.shape[1]) + as_column(bt, old.shape[0]) * old
    rows[...] = r
    weighted = r * weights[...]
    put_pieces(out, dot(weighted, grads[...], ((1,), (0,))), col(weighted * r))


def last_step(base, resid, norm, square, beta, arrived, alpha, out):
    tiles = summed(arrived)
    a = norm[...] / (row_in(tiles[-1], 0) + DAMPING * square[...])
    alpha[...] = a
    first = own_first()
    line = resid[...] + as_column(beta[...], LINES, first) * own_lines(base)
    image = body_of(tiles[:-1], base.shape[1])
    r = resid[...] - as_column(a, LINES, first) * (image + DAMPING * line)
    put_copies(out, tiles_of(r))


def outputs(
    scale, base, resid, beta, alpha0, alpha1, rows0, rows1, arrived, scores, answer, last, *scratch
):
    score_held, answer_held, last_held, sems = scratch
    last_held[...] = laid_out(arrived, base.shape[1])
    stores = [
        pltpu.make_async_copy(held, out, sems.at[i])
        for i, (held, out) in enumerate(
            ((last_held, last), (answer_held, answer), (score_held, scores))
        )
    ]
    stores[0].start()
    b = base[...]
    dirs = b.shape[0]
    a0, a1 = as_column(alpha0[...], dirs), as_column(alpha1[...], dirs)
    answer_held[...] = a0 * b + a1 * (resid[...] + as_column(beta[...], dirs) * b)
    stores[1].start()
    every = (a0 * rows0[...] + a1 * rows1[...]) * scale
    share = scores.shape[0]
    feat = lax.axis_index("feat")
    mine = every[:, :share]
    for i in range(1, every.shape[1] // share):
        mine = jnp.where(feat == i, every[:, i * share : (i + 1) * share], mine)
    score_held[...] = mine.T
    stores[2].start()
    for store in stores:
        store.wait()


VMEM = pl.BlockSpec(memory_space=pltpu.VMEM)
HBM = pl.BlockSpec(memory_space=pltpu.HBM)


def call(kernel, outs, *args, inputs=VMEM, results=VMEM, scratch=()):
    return pl.pallas_call(
        kernel,
        out_shape=[jax.ShapeDtypeStruct(s, t) for s, t in outs],
        in_specs=[inputs] * len(args),
        out_specs=[results] * len(outs),
        scratch_shapes=list(scratch),
        compiler_params=pltpu.CompilerParams(vmem_limit_bytes=8 * 2**20),
    )(*args)


def exchanged(pieces, axis, groups):
    return lax.all_to_all(pieces, axis, 0, 0, tiled=True, axis_index_groups=groups)


def per_device(grads, weights, targets):
    n_samp, n_feat = lax.axis_size("samp"), lax.axis_size("feat")
    samples = grads.shape[0]
    share = samples // n_feat
    scaled = (weights / (samples * n_samp))[None, :]
    base = targets.T
    dirs, m = base.shape
    across = m // LANES
    row_tiles = dirs // LINES * (samples // LANES) + 1
    block, row, part = ((dirs, m), F32), ((1, LANES), F32), ((LINES, m), F32)
    block_rows = ((dirs, samples), F32)
    to_x = ((COLUMNS, row_tiles, LINES, LANES), BF16)
    to_half = ((row_tiles, LINES, LANES), BF16)
    to_near = ((NEAR, across + 1, LINES, LANES), BF16)
    to_far = ((LAYERS, across + 1, LINES, LANES), BF16)
    to_all = ((NEAR, across, LINES, LANES), BF16)

    out, grads, base = call(
        first_rows,
        [to_x, (grads.shape, grads.dtype), block],
        pltpu.with_memory_space_constraint(grads, pltpu.HBM),
        pltpu.with_memory_space_constraint(base, pltpu.HBM),
        inputs=HBM,
        scratch=[pltpu.SemaphoreType.DMA((2,))],
    )
    (mine,) = call(functools.partial(x_total, 1), [to_half], exchanged(out, "feat", X_GROUPS))
    other = lax.ppermute(mine, "feat", SWAP)
    rows0, norm0, out = call(
        first_image, [block_rows, row, to_near], grads, scaled, mine, other
    )
    (out,) = call(near_total, [to_far], exchanged(out, "samp", NEAR_GROUPS))
    resid_own, alpha0, out = call(
        first_step, [part, row, to_all], base, norm0, exchanged(out, "samp", FAR_GROUPS)
    )
    resid, out = call(
        next_rows, [block, to_x], grads, base, exchanged(out, "samp", NEAR_GROUPS)
    )
    (mine,) = call(functools.partial(x_total, 2), [to_half], exchanged(out, "feat", X_GROUPS))
    other = lax.ppermute(mine, "feat", SWAP)
    rows1, norm1, square, beta, out = call(
        next_image,
        [block_rows, row, row, row, to_near],
        grads,
        scaled,
        mine,
        other,
        rows0,
        norm0,
    )
    (out,) = call(near_total, [to_far], exchanged(out, "samp", NEAR_GROUPS))
    alpha1, out = call(
        last_step,
        [row, to_all],
        base,
        resid_own,
        norm1,
        square,
        beta,
        exchanged(out, "samp", FAR_GROUPS),
    )
    scores, answer, last = call(
        functools.partial(outputs, 1.0 / math.sqrt(m * n_feat)),
        [((share, dirs), F32), block, block],
        base,
        resid,
        beta,
        alpha0,
        alpha1,
        rows0,
        rows1,
        exchanged(out, "samp", NEAR_GROUPS),
        results=HBM,
        scratch=[
            pltpu.VMEM((share, dirs), F32),
            pltpu.VMEM((dirs, m), F32),
            pltpu.VMEM((dirs, m), F32),
            pltpu.SemaphoreType.DMA((3,)),
        ],
    )
    return scores, answer.T, last.T


def solution(mesh):
    return jax.shard_map(
        per_device,
        mesh=mesh,
        in_specs=(P("samp", "feat"), P("samp"), P("feat", None)),
        out_specs=(P(("samp", "feat"), None), P("feat", None), P("feat", None)),
        check_vma=False,
    )
```

```python
import functools
import math

import jax
import jax.numpy as jnp
from jax import lax
from jax.experimental import pallas as pl
from jax.experimental.pallas import tpu as pltpu
from jax.sharding import PartitionSpec as P

DAMPING = 0.1
PLANES, LAYERS, CORES = 4, 8, 2
HALVES, COLUMNS = 2, 4
NEAR = PLANES * CORES
LINES, LANES = 8, 128

X_GROUPS = [[h * COLUMNS + i for i in range(COLUMNS)] for h in range(HALVES)]
SWAP = [(i, (i + COLUMNS) % (HALVES * COLUMNS)) for i in range(HALVES * COLUMNS)]
FAR_ORDER = (3, 7, 0, 6, 1, 5, 2, 4)
NEAR_ORDER = ((1, 1), (2, 0), (1, 0), (2, 1), (0, 1), (3, 0), (0, 0), (3, 1))
NEAR_GROUPS = [[(y * LAYERS + z) * CORES + c for y, c in NEAR_ORDER] for z in range(LAYERS)]
FAR_GROUPS = [
    [(y * LAYERS + z) * CORES + c for z in FAR_ORDER] for y in range(PLANES) for c in range(CORES)
]
F32, BF16 = jnp.float32, jnp.bfloat16


def dot(a, b, dims):
    return lax.dot_general(a.astype(BF16), b, (dims, ((), ())), preferred_element_type=F32)


def col(x):
    return jnp.sum(x, axis=1, keepdims=True)


def iota(shape, axis):
    return lax.broadcasted_iota(jnp.int32, shape, axis)


def as_row(column):
    shape = (column.shape[0], LANES)
    eye = iota(shape, 0) == iota(shape, 1)
    return jnp.sum(jnp.where(eye, jnp.broadcast_to(column, shape), 0.0), axis=0, keepdims=True)


def as_column(row, n, first=0):
    shape = (n, LANES)
    eye = iota(shape, 0) + first == iota(shape, 1)
    return col(jnp.where(eye, jnp.broadcast_to(row, shape), 0.0))


def tail_of(*rows):
    shape = (LINES, LANES)
    tail = jnp.zeros(shape, F32)
    for i, x in enumerate(rows):
        x = jnp.broadcast_to(x, shape)
        for term in range(3):
            part = x.astype(BF16).astype(F32)
            tail = jnp.where(iota(shape, 0) == 3 * i + term, part, tail)
            x = x - part
    return tail


def row_in(tail, i):
    line = iota(tail.shape, 0)
    chosen = (line >= 3 * i) & (line < 3 * i + 3)
    return jnp.sum(jnp.where(chosen, tail, 0.0), axis=0, keepdims=True)


def tiles_of(body):
    return [
        body[i : i + LINES, j : j + LANES]
        for i in range(0, body.shape[0], LINES)
        for j in range(0, body.shape[1], LANES)
    ]


def body_of(tiles, width):
    across = width // LANES
    lines = [
        jnp.concatenate(tiles[i : i + across], axis=1) for i in range(0, len(tiles), across)
    ]
    return jnp.concatenate(lines, axis=0) if len(lines) > 1 else lines[0]


def put(ref, tiles):
    for i, tile in enumerate(tiles):
        ref[i] = tile.astype(BF16)


def put_copies(ref, tiles):
    for i in range(ref.shape[0]):
        put(ref.at[i], tiles)


def tiles_in(ref):
    return [ref[i].astype(F32) for i in range(ref.shape[0])]


def summed(ref):
    totals = tiles_in(ref.at[0])
    for i in range(1, ref.shape[0]):
        totals = [a + b for a, b in zip(totals, tiles_in(ref.at[i]))]
    return totals


def own_first():
    me = lax.axis_index("samp")
    y, c = me // (LAYERS * CORES), lax.rem(me, CORES)
    first = jnp.int32(0)
    for place, (plane, core) in enumerate(NEAR_ORDER):
        first = jnp.where((y == plane) & (c == core), place * LINES, first)
    return first


def own_lines(ref):
    return ref[pl.ds(pl.multiple_of(own_first(), LINES), LINES), :]


def put_pieces(out, image, curve):
    tiles, tail = tiles_of(image), tail_of(as_row(curve))
    across = len(tiles) // out.shape[0]
    for i in range(out.shape[0]):
        put(out.at[i], tiles[i * across : (i + 1) * across] + [tail])


def first_rows(grads, base, out, held, line, sems):
    loads = [
        pltpu.make_async_copy(base, line, sems.at[0]),
        pltpu.make_async_copy(grads, held, sems.at[1]),
    ]
    for load in loads:
        load.start()
    loads[0].wait()
    b = line[...]
    tail = tail_of(as_row(col(b * b)))
    packed = b.astype(BF16)
    loads[1].wait()
    put_copies(out, tiles_of(dot(packed, held[...], ((1,), (1,)))) + [tail])


def x_total(count, arrived, out):
    tiles = summed(arrived)
    tail = tail_of(*[row_in(tiles[-1], i) for i in range(count)])
    put(out, tiles[:-1] + [tail])


def first_image(grads, weights, mine, other, rows, norm, out):
    tiles = [a + b for a, b in zip(tiles_in(mine), tiles_in(other))]
    r = body_of(tiles[:-1], rows.shape[1])
    rows[...] = r
    norm[...] = row_in(tiles[-1], 0)
    weighted = r * weights[...]
    put_pieces(out, dot(weighted, grads[...], ((1,), (0,))), col(weighted * r))


def near_total(arrived, out):
    tiles = summed(arrived)
    put_copies(out, tiles[:-1] + [tail_of(row_in(tiles[-1], 0))])


def first_step(base, norm, arrived, resid, alpha, out):
    tiles = summed(arrived)
    n = norm[...]
    a = n / (row_in(tiles[-1], 0) + DAMPING * n)
    alpha[...] = a
    b = own_lines(base)
    image = body_of(tiles[:-1], base.shape[1])
    r = b - as_column(a, LINES, own_first()) * (image + DAMPING * b)
    resid[...] = r
    put_copies(out, tiles_of(r))


def laid_out(arrived, width):
    return body_of([t for i in range(arrived.shape[0]) for t in tiles_in(arrived.at[i])], width)


def next_rows(grads, base, arrived, resid, out):
    b = base[...]
    r = laid_out(arrived, b.shape[1])
    resid[...] = r
    tail = tail_of(as_row(col(r * r)), as_row(col(r * b)))
    put_copies(out, tiles_of(dot(r, grads[...], ((1,), (1,)))) + [tail])


def next_image(grads, weights, mine, other, rows0, norm0, rows, norm, square, beta, out):
    tiles = [a + b for a, b in zip(tiles_in(mine), tiles_in(other))]
    n0, n1, cross = norm0[...], row_in(tiles[-1], 0), row_in(tiles[-1], 1)
    bt = n1 / n0
    norm[...] = n1
    beta[...] = bt
    square[...] = n1 + 2.0 * bt * cross + bt * bt * n0
    old = rows0[...]
    r = body_of(tiles[:-1], old.shape[1]) + as_column(bt, old.shape[0]) * old
    rows[...] = r
    weighted = r * weights[...]
    put_pieces(out, dot(weighted, grads[...], ((1,), (0,))), col(weighted * r))


def last_step(base, resid, norm, square, beta, arrived, alpha, out):
    tiles = summed(arrived)
    a = norm[...] / (row_in(tiles[-1], 0) + DAMPING * square[...])
    alpha[...] = a
    first = own_first()
    line = resid[...] + as_column(beta[...], LINES, first) * own_lines(base)
    image = body_of(tiles[:-1], base.shape[1])
    r = resid[...] - as_column(a, LINES, first) * (image + DAMPING * line)
    put_copies(out, tiles_of(r))


def outputs(
    scale, base, resid, beta, alpha0, alpha1, rows0, rows1, arrived, scores, answer, last, *scratch
):
    score_held, answer_held, last_held, sems = scratch
    last_held[...] = laid_out(arrived, base.shape[1])
    stores = [
        pltpu.make_async_copy(held, out, sems.at[i])
        for i, (held, out) in enumerate(
            ((last_held, last), (answer_held, answer), (score_held, scores))
        )
    ]
    stores[0].start()
    b = base[...]
    dirs = b.shape[0]
    a0, a1 = as_column(alpha0[...], dirs), as_column(alpha1[...], dirs)
    answer_held[...] = a0 * b + a1 * (resid[...] + as_column(beta[...], dirs) * b)
    stores[1].start()
    every = (a0 * rows0[...] + a1 * rows1[...]) * scale
    share = scores.shape[0]
    feat = lax.axis_index("feat")
    mine = every[:, :share]
    for i in range(1, every.shape[1] // share):
        mine = jnp.where(feat == i, every[:, i * share : (i + 1) * share], mine)
    score_held[...] = mine.T
    stores[2].start()
    for store in stores:
        store.wait()


VMEM = pl.BlockSpec(memory_space=pltpu.VMEM)
HBM = pl.BlockSpec(memory_space=pltpu.HBM)


def call(kernel, outs, *args, inputs=VMEM, results=VMEM, scratch=()):
    return pl.pallas_call(
        kernel,
        out_shape=[jax.ShapeDtypeStruct(s, t) for s, t in outs],
        in_specs=[inputs] * len(args),
        out_specs=[results] * len(outs),
        scratch_shapes=list(scratch),
        compiler_params=pltpu.CompilerParams(vmem_limit_bytes=8 * 2**20),
    )(*args)


def exchanged(pieces, axis, groups):
    return lax.all_to_all(pieces, axis, 0, 0, tiled=True, axis_index_groups=groups)


def per_device(grads, weights, targets):
    n_samp, n_feat = lax.axis_size("samp"), lax.axis_size("feat")
    samples = grads.shape[0]
    share = samples // n_feat
    scaled = (weights / (samples * n_samp))[None, :]
    base = targets.T
    dirs, m = base.shape
    across = m // LANES
    row_tiles = dirs // LINES * (samples // LANES) + 1
    block, row, part = ((dirs, m), F32), ((1, LANES), F32), ((LINES, m), F32)
    block_rows = ((dirs, samples), F32)
    to_x = ((COLUMNS, row_tiles, LINES, LANES), BF16)
    to_half = ((row_tiles, LINES, LANES), BF16)
    to_near = ((NEAR, across + 1, LINES, LANES), BF16)
    to_far = ((LAYERS, across + 1, LINES, LANES), BF16)
    to_all = ((NEAR, across, LINES, LANES), BF16)

    out, grads, base = call(
        first_rows,
        [to_x, (grads.shape, grads.dtype), block],
        pltpu.with_memory_space_constraint(grads, pltpu.HBM),
        pltpu.with_memory_space_constraint(base, pltpu.HBM),
        inputs=HBM,
        scratch=[pltpu.SemaphoreType.DMA((2,))],
    )
    (mine,) = call(functools.partial(x_total, 1), [to_half], exchanged(out, "feat", X_GROUPS))
    other = lax.ppermute(mine, "feat", SWAP)
    rows0, norm0, out = call(
        first_image, [block_rows, row, to_near], grads, scaled, mine, other
    )
    (out,) = call(near_total, [to_far], exchanged(out, "samp", NEAR_GROUPS))
    resid_own, alpha0, out = call(
        first_step, [part, row, to_all], base, norm0, exchanged(out, "samp", FAR_GROUPS)
    )
    resid, out = call(
        next_rows, [block, to_x], grads, base, exchanged(out, "samp", NEAR_GROUPS)
    )
    (mine,) = call(functools.partial(x_total, 2), [to_half], exchanged(out, "feat", X_GROUPS))
    other = lax.ppermute(mine, "feat", SWAP)
    rows1, norm1, square, beta, out = call(
        next_image,
        [block_rows, row, row, row, to_near],
        grads,
        scaled,
        mine,
        other,
        rows0,
        norm0,
    )
    (out,) = call(near_total, [to_far], exchanged(out, "samp", NEAR_GROUPS))
    alpha1, out = call(
        last_step,
        [row, to_all],
        base,
        resid_own,
        norm1,
        square,
        beta,
        exchanged(out, "samp", FAR_GROUPS),
    )
    scores, answer, last = call(
        functools.partial(outputs, 1.0 / math.sqrt(m * n_feat)),
        [((share, dirs), F32), block, block],
        base,
        resid,
        beta,
        alpha0,
        alpha1,
        rows0,
        rows1,
        exchanged(out, "samp", NEAR_GROUPS),
        results=HBM,
        scratch=[
            pltpu.VMEM((share, dirs), F32),
            pltpu.VMEM((dirs, m), F32),
            pltpu.VMEM((dirs, m), F32),
            pltpu.SemaphoreType.DMA((3,)),
        ],
    )
    return scores, answer.T, last.T


def solution(mesh):
    return jax.shard_map(
        per_device,
        mesh=mesh,
        in_specs=(P("samp", "feat"), P("samp"), P("feat", None)),
        out_specs=(P(("samp", "feat"), None), P("feat", None), P("feat", None)),
        check_vma=False,
    )
```
